32 devices in a mesh: phase: 2 (over x), seq: 16 (over z, y, core).
Axes of the slice: x: 2, y: 2, z: 4, core: 2. Of those that a mesh axis runs over, the one named last changes fastest.
Arguments:
- dec_in: bfloat16 [2, 512, 4096], P(None, None, 'seq'), may hold values from -6 to 6
- enc_kv: bfloat16 [2, 2, 2048, 8192], P('phase', None, 'seq'), may hold values from -15 to 15
- dec_seg: int32 [2, 512], replicated, may hold values from 0 to 3, never falling along the last dimension, each value on 1 to 256 neighbouring positions
- enc_seg: int32 [2, 2048], replicated, may hold values from 0 to 3, never falling along the last dimension, each value on 1 to 1024 neighbouring positions
- q_gain: float32 [2, 4096], P('phase', 'seq'), may hold values from 0.5 to 1.5
- o_gain: float32 [2, 4096], P('phase', 'seq'), may hold values from 1 to 8
- cotangent: bfloat16 [2, 512, 4096], P(None, None, 'seq'), may hold values from -6 to 6
Outputs:
- sect_out: bfloat16 [2, 2, 512, 4096], P('phase', None, None, 'seq')
- grad_kv: bfloat16 [2, 2, 2048, 8192], P('phase', None, 'seq')
- grad_q_gain: float32 [2, 4096], P('phase', 'seq')
- grad_o_gain: float32 [2, 4096], P('phase', 'seq')
The draws below stay inside these ranges and needn't reach their ends.
Inputs may be any that keep to these rules, and one draw needn't show every extreme that they name: `dec_seg`: every one of the 4 documents has positions in both the decoder and the encoder of each micro-batch.
All inputs are finite; a program needn't handle non-finite values.
Results may differ from the reference program's by a relative error of at most 0.0075.
The reference program's roundings to bfloat16 on the way count: a program that leaves them out, or rounds other values in their place, can miss the bound.
Values may be sent and summed in bfloat16 or wider, within the bound.
A program may use at most 192 MiB of HBM per device.

```python
import math
import jax
import jax.numpy as jnp
import numpy as np
from jax import lax

D = 4096
HEADS = 64
HEAD = 64
DEC_TOK = 512
MICRO = 2
DOCS = 4
ENC_TOK = 2048
SECTIONS = 2


def steps_of(key, extent, cuts, smallest, top_value):
    loudness = 1.0
    for position, parts in cuts:
        steps = jax.random.uniform(jax.random.fold_in(jax.random.fold_in(key, 6), position), (parts,), jnp.float32, smallest / len(cuts), top_value / len(cuts))
        loudness = loudness * jnp.repeat(jnp.exp(steps), extent[position] // parts).reshape((-1,) + (1,) * (len(extent) - 1 - position))
    return loudness


def profile(count, total, bound, slope):
    portions = [(1 << 20) // math.isqrt(rank ** slope) + 1 for rank in range(2, count + 1)]
    rest, counts = total - bound - (count - 1), [1] * (count - 1)
    while rest > 0:
        candidates = [i for i in range(count - 1) if counts[i] < bound]
        whole, left = sum([portions[i] for i in candidates]), rest
        for i in candidates:
            extra = min(bound - counts[i], max(1, left * portions[i] // whole), rest)
            counts[i] = counts[i] + extra
            rest = rest - extra
    return np.array([bound] + counts)


def uneven(key, amount, total, bound, skew):
    if amount == 2:
        one = jax.random.randint(key, (), max(1, total - bound), min(bound, total - 1) + 1)
        return jnp.stack([one, total - one])
    tallies = jnp.asarray(profile(amount, total, bound, skew), jnp.int32)
    pairs = (amount - 1) // 2
    source_of, taker = tallies[1:1 + 2 * pairs:2], tallies[2:2 + 2 * pairs:2]
    room = jnp.minimum(source_of - 1, bound - taker)
    passed = jax.random.randint(jax.random.fold_in(key, 1), (pairs,), 0, 1 << 20) % (room + 1)
    tallies = tallies.at[1:1 + 2 * pairs:2].set(source_of - passed).at[2:2 + 2 * pairs:2].set(taker + passed)
    return tallies[jax.random.permutation(jax.random.fold_in(key, 2), amount)]


def scatter_about(key, dims, spread, limit, cuts=(), kind=jnp.bfloat16):
    result = jax.random.normal(key, dims, jnp.float32) * spread
    if len(cuts) > 0:
        result = steps_of(key, dims, cuts, -0.22, 0.18) * result
    return jnp.clip(result, min=-limit, max=limit).astype(kind)


def setup_inputs(seed: int = 0) -> dict:
    seeds = jax.random.split(jax.random.key(seed), 8)
    dec_in = scatter_about(seeds[0], (MICRO, DEC_TOK, D), 1.0, 6.0, ((2, 16),))
    enc_kv = scatter_about(seeds[1], (SECTIONS, MICRO, ENC_TOK, 2 * D), 2.5, 15.0, ((0, 2), (2, 16)))
    dec_seg = jax.vmap(lambda own: jnp.searchsorted(jnp.cumsum(uneven(own, DOCS, DEC_TOK, DEC_TOK // 2, 2)), jnp.arange(DEC_TOK), side="right"))(jax.random.split(seeds[2], MICRO)).reshape((MICRO, DEC_TOK)).astype(jnp.int32)
    enc_seg = jax.vmap(lambda own: jnp.searchsorted(jnp.cumsum(uneven(own, DOCS, ENC_TOK, ENC_TOK // 2, 2)), jnp.arange(ENC_TOK), side="right"))(jax.random.split(seeds[3], MICRO)).reshape((MICRO, ENC_TOK)).astype(jnp.int32)
    q_gain = jnp.clip(1.0 + 0.1 * jax.random.normal(seeds[4], (SECTIONS, D), jnp.float32), 0.5, 1.5)
    o_gain = jnp.clip(jnp.exp(math.log(8.0) - 2.0794415 * jax.random.uniform(seeds[5], (SECTIONS, D), jnp.float32) ** steps_of(seeds[5], (SECTIONS, D), ((0, 2), (1, 16)), -0.2, 0.2)), 1.0, 8.0)
    cotangent = scatter_about(seeds[6], (MICRO, DEC_TOK, D), 1.0, 6.0, ((2, 16),))
    return dict(dec_in=dec_in, enc_kv=enc_kv, dec_seg=dec_seg, enc_seg=enc_seg, q_gain=q_gain, o_gain=o_gain, cotangent=cotangent)


eps = 1e-06
neg_big = -1e+30

def head_forward(query, keys, values, allowed):
    scale = 1.0 / math.sqrt(HEAD)
    scores = jnp.dot(query, keys.T, preferred_element_type=jnp.float32) * scale
    scores = jnp.where(allowed, scores, neg_big)
    top = lax.optimization_barrier(jnp.max(scores, axis=1, keepdims=True))
    expo = jnp.exp(scores - top)
    probs = expo / lax.optimization_barrier(jnp.sum(expo, axis=1, keepdims=True))
    weights = probs.astype(jnp.bfloat16)
    output = jnp.dot(weights, values, preferred_element_type=jnp.float32)
    return (output, probs, weights)

def head_backward(query, keys, values, allowed, grad_out):
    scale = 1.0 / math.sqrt(HEAD)
    output, probs, weights = head_forward(query, keys, values, allowed)
    grad_low = grad_out.astype(jnp.bfloat16)
    grad_values = jnp.dot(weights.T, grad_low, preferred_element_type=jnp.float32)
    grad_probs = jnp.dot(grad_low, values.T, preferred_element_type=jnp.float32)
    delta = lax.optimization_barrier(jnp.sum(probs * grad_probs, axis=1, keepdims=True))
    grad_scores = (probs * (grad_probs - delta) * scale).astype(jnp.bfloat16)
    grad_query = jnp.dot(grad_scores, keys, preferred_element_type=jnp.float32)
    grad_keys = jnp.dot(grad_scores.T, query, preferred_element_type=jnp.float32)
    return (output, grad_query, grad_keys, grad_values)

def prepare(x, qgain):
    xf = x.astype(jnp.float32)
    total = lax.optimization_barrier(jnp.sum(xf * xf, axis=1))
    inv = lax.rsqrt(total / D + eps)
    normed = xf * inv[:, None]
    query = (normed * qgain[None, :]).astype(jnp.bfloat16)
    return (xf, inv, normed, query)

def by_heads(array):
    return jnp.transpose(array.reshape(array.shape[0], HEADS, HEAD), (1, 0, 2))

def section_forward(x, keyval, allowed, qgain, ogain):
    xf, inv, normed, query = prepare(x, qgain)
    keys = jnp.transpose(keyval[:, :, 0, :], (1, 0, 2))
    values = jnp.transpose(keyval[:, :, 1, :], (1, 0, 2))

    def one_head(item):
        return head_forward(item[0], item[1], item[2], allowed)[0]
    output = lax.map(one_head, (by_heads(query), keys, values))
    output = jnp.transpose(output, (1, 0, 2)).reshape(x.shape[0], D)
    return (xf + ogain[None, :] * output).astype(jnp.bfloat16)

def section_backward(x, keyval, allowed, qgain, ogain, grad_y):
    xf, inv, normed, query = prepare(x, qgain)
    keys = jnp.transpose(keyval[:, :, 0, :], (1, 0, 2))
    values = jnp.transpose(keyval[:, :, 1, :], (1, 0, 2))
    grad_f = grad_y.astype(jnp.float32)
    grad_out = grad_f * ogain[None, :]

    def one_head(item):
        return head_backward(item[0], item[1], item[2], allowed, item[3])
    output, grad_query, grad_keys, grad_values = lax.map(one_head, (by_heads(query), keys, values, by_heads(grad_out)))
    rows = x.shape[0]
    output = jnp.transpose(output, (1, 0, 2)).reshape(rows, D)
    grad_query = jnp.transpose(grad_query, (1, 0, 2)).reshape(rows, D)
    grad_pair = jnp.transpose(jnp.stack([grad_keys, grad_values], axis=2), (1, 0, 2, 3))
    grad_pair = grad_pair.reshape(grad_pair.shape[0], 2 * D).astype(jnp.bfloat16)
    grad_qg = lax.optimization_barrier(jnp.sum(grad_query * normed, axis=0))
    grad_og = lax.optimization_barrier(jnp.sum(grad_f * output, axis=0))
    grad_normed = grad_query * qgain[None, :]
    cross = lax.optimization_barrier(jnp.sum(grad_normed * xf, axis=1))
    grad_x = grad_f + inv[:, None] * grad_normed - xf * (inv * inv * inv)[:, None] * (cross / D)[:, None]
    return (grad_x.astype(jnp.bfloat16), grad_pair, grad_qg, grad_og)

def reference(dec_in, enc_kv, dec_seg, enc_seg, q_gain, o_gain, cotangent):
    outs = [[None] * MICRO for s in range(SECTIONS)]
    inputs = [[None] * MICRO for s in range(SECTIONS)]
    for m in range(MICRO):
        allowed = dec_seg[m][:, None] == enc_seg[m][None, :]
        x = dec_in[m]
        for s in range(SECTIONS):
            keyval = enc_kv[s, m].reshape(ENC_TOK, HEADS, 2, HEAD)
            inputs[s][m] = x
            x = section_forward(x, keyval, allowed, q_gain[s], o_gain[s])
            outs[s][m] = x
    grads = [[None] * MICRO for s in range(SECTIONS)]
    qg_sum = [jnp.zeros((D,), jnp.float32) for s in range(SECTIONS)]
    og_sum = [jnp.zeros((D,), jnp.float32) for s in range(SECTIONS)]
    for m in range(MICRO):
        allowed = dec_seg[m][:, None] == enc_seg[m][None, :]
        grad_y = cotangent[m]
        for s in reversed(range(SECTIONS)):
            keyval = enc_kv[s, m].reshape(ENC_TOK, HEADS, 2, HEAD)
            grad_y, grad_pair, grad_qg, grad_og = section_backward(inputs[s][m], keyval, allowed, q_gain[s], o_gain[s], grad_y)
            grads[s][m] = grad_pair
            qg_sum[s] = qg_sum[s] + grad_qg
            og_sum[s] = og_sum[s] + grad_og
    sect_out = jnp.stack([jnp.stack(outs[s]) for s in range(SECTIONS)])
    grad_kv = jnp.stack([jnp.stack(grads[s]) for s in range(SECTIONS)])
    return (sect_out, grad_kv, jnp.stack(qg_sum), jnp.stack(og_sum))
```

```python
import functools

import jax
import jax.numpy as jnp
from jax import lax
from jax.experimental import pallas as pl
from jax.experimental.pallas import tpu as pltpu
from jax.sharding import PartitionSpec as P

HEAD = 64
QROWS = 256
CHUNK = 256
SCALE = 0.125

eps = 1e-06
neg_big = -1e30
MESH = pl.DeviceIdType.MESH
VMEM_BYTES = 56 * 1024 * 1024


def matmul(a, b):
    return lax.dot_general(a, b, (((1,), (0,)), ((), ())), preferred_element_type=jnp.float32)


def matmul_t(a, b):
    return lax.dot_general(a, b, (((1,), (1,)), ((), ())), preferred_element_type=jnp.float32)


def attention_kernel(backward, active, width, *refs):
    if backward:
        (phase_ref, bound_ref, kv_ref, kseg_ref, qseg_ref, x_ref, total_ref, qg_ref, og_ref, g_ref,
         y_ref, gkv_ref, part_ref, cross_ref, gqg_ref, gog_ref,
         score_ref, top_ref, kvt_ref, pair_ref, gprob_ref, acc_ref) = refs
    else:
        (phase_ref, bound_ref, kv_ref, kseg_ref, qseg_ref, x_ref, total_ref, qg_ref, og_ref,
         y_ref, score_ref, top_ref, kvt_ref, pair_ref) = refs
    enc = kv_ref.shape[0]
    feats, rows = x_ref.shape
    heads = feats // HEAD
    block = min(QROWS, rows)
    chunk = min(CHUNK, enc)
    every = range(heads)
    lanes = [slice(2 * HEAD * h, 2 * HEAD * (h + 1)) for h in every]
    owns = [slice(HEAD * h, HEAD * (h + 1)) for h in every]

    def place(c):
        return pl.ds(pl.multiple_of(c * chunk, chunk), chunk)

    def work():
        def turn(c, _):
            at = place(c)
            for h in every:
                kvt_ref[h, :, at] = kv_ref[at, lanes[h]].T
                if backward:
                    acc_ref[h, at, :] = jnp.zeros((chunk, 2 * HEAD), jnp.float32)
            return 0

        lax.fori_loop(0, enc // chunk, turn, 0)
        row = jnp.zeros((1, block), jnp.float32)
        tall = jnp.zeros((2 * HEAD, block), jnp.float32)
        blank = jnp.zeros((HEAD, block), jnp.bfloat16)
        for b in range(rows // block):
            cols = slice(b * block, (b + 1) * block)
            low = bound_ref[2 * b]
            high = bound_ref[2 * b + 1]
            inv = lax.rsqrt(total_ref[:, cols] / width + eps)
            qseg = qseg_ref[:, cols]

            def normed_of(h):
                return x_ref[owns[h], cols].astype(jnp.float32) * inv

            for h in every:
                query = (normed_of(h) * qg_ref[owns[h], :]).astype(jnp.bfloat16)
                scaled = (query.astype(jnp.float32) * SCALE).astype(jnp.bfloat16)
                pair_ref[h, :, :block] = jnp.concatenate([scaled, blank], axis=0)
                if backward:
                    grad = (g_ref[owns[h], cols].astype(jnp.float32) * og_ref[owns[h], :]).astype(jnp.bfloat16)
                    pair_ref[h, :, block:] = jnp.concatenate([blank, grad], axis=0)

            def scores(c, carry):
                at = place(c)
                allowed = kseg_ref[at, :] == qseg
                found = []
                for h in every:
                    top, total = carry[h]
                    s = matmul(kv_ref[at, lanes[h]], pair_ref[h, :, :block])
                    s = jnp.where(allowed, s, neg_big)
                    higher = jnp.maximum(top, jnp.max(s, axis=0, keepdims=True))
                    e = jnp.exp(s - higher)
                    score_ref[h, at, :] = e
                    top_ref[h, pl.ds(c, 1), :] = higher
                    found.append((higher, total * jnp.exp(top - higher) + jnp.sum(e, axis=0, keepdims=True)))
                return tuple(found)

            found = lax.fori_loop(low, high, scores, tuple((row + neg_big, row) for h in every))
            tops = [top for top, _ in found]
            shares = [1.0 / total for _, total in found]

            def probs_of(h, c, at):
                return score_ref[h, at, :] * (jnp.exp(top_ref[h, pl.ds(c, 1), :] - tops[h]) * shares[h])

            if not backward:
                def outputs(c, outs):
                    at = place(c)
                    return tuple(
                        outs[h] + matmul(kvt_ref[h, :, at], probs_of(h, c, at).astype(jnp.bfloat16)) for h in every
                    )

                outs = lax.fori_loop(low, high, outputs, tuple(tall for h in every))
                for h in every:
                    xf = x_ref[owns[h], cols].astype(jnp.float32)
                    y_ref[owns[h], cols] = (xf + og_ref[owns[h], :] * outs[h][HEAD:]).astype(jnp.bfloat16)
                continue

            def outputs_and_delta(c, carry):
                at = place(c)
                found = []
                for h in every:
                    out, delta = carry[h]
                    probs = probs_of(h, c, at)
                    score_ref[h, at, :] = probs
                    gprob = matmul(kv_ref[at, lanes[h]], pair_ref[h, :, block:])
                    gprob_ref[h, at, :] = gprob
                    out = out + matmul(kvt_ref[h, :, at], probs.astype(jnp.bfloat16))
                    found.append((out, delta + jnp.sum(probs * gprob, axis=0, keepdims=True)))
                return tuple(found)

            found = lax.fori_loop(low, high, outputs_and_delta, tuple((tall, row) for h in every))
            outs = [out for out, _ in found]
            deltas = [delta for _, delta in found]

            def gradients(c, gqs):
                at = place(c)
                found = []
                for h in every:
                    probs = score_ref[h, at, :]
                    gscore = (probs * (gprob_ref[h, at, :] - deltas[h])).astype(jnp.bfloat16)
                    both = jnp.concatenate([gscore, probs.astype(jnp.bfloat16)], axis=1)
                    acc_ref[h, at, :] += matmul_t(both, pair_ref[h])
                    found.append(gqs[h] + matmul(kvt_ref[h, :, at], gscore))
                return tuple(found)

            gqs = lax.fori_loop(low, high, gradients, tuple(tall for h in every))
            cross = row
            for h in every:
                own = owns[h]
                xf = x_ref[own, cols].astype(jnp.float32)
                gf = g_ref[own, cols].astype(jnp.float32)
                out = outs[h][HEAD:]
                gq = gqs[h][:HEAD] * SCALE
                gn = gq * qg_ref[own, :]
                y_ref[own, cols] = (xf + og_ref[own, :] * out).astype(jnp.bfloat16)
                part_ref[own, cols] = gf + inv * gn
                cross = cross + jnp.sum(gn * xf, axis=0, keepdims=True)
                gqg = jnp.sum(gq * normed_of(h), axis=1, keepdims=True)
                gog = jnp.sum(gf * out, axis=1, keepdims=True)
                gqg_ref[own, :] = gqg if b == 0 else gqg_ref[own, :] + gqg
                gog_ref[own, :] = gog if b == 0 else gog_ref[own, :] + gog
            cross_ref[:, cols] = cross
        if backward:
            def store(c, _):
                at = place(c)
                for h in every:
                    gkv_ref[at, lanes[h]] = acc_ref[h, at, :].astype(jnp.bfloat16)
                return 0

            lax.fori_loop(0, enc // chunk, store, 0)

    pl.when(phase_ref[0] == active)(work)


def attention(backward, active, width, phase, bounds, kv, kseg, qseg, x, total, qg, og, g=None):
    enc = kv.shape[0]
    feats, rows = x.shape
    block = min(QROWS, rows)
    shapes = [jax.ShapeDtypeStruct((feats, rows), jnp.bfloat16)]
    heads = feats // HEAD
    scratch = [
        pltpu.VMEM((heads, enc, block), jnp.float32),
        pltpu.VMEM((heads, max(8, enc // min(CHUNK, enc)), block), jnp.float32),
        pltpu.VMEM((heads, 2 * HEAD, enc), jnp.bfloat16),
        pltpu.VMEM((heads, 2 * HEAD, 2 * block if backward else block), jnp.bfloat16),
    ]
    operands = [phase, bounds, kv, kseg, qseg, x, total, qg, og]
    if backward:
        operands.append(g)
        shapes += [
            jax.ShapeDtypeStruct(kv.shape, jnp.bfloat16),
            jax.ShapeDtypeStruct((feats, rows), jnp.float32),
            jax.ShapeDtypeStruct((1, rows), jnp.float32),
            jax.ShapeDtypeStruct((feats, 1), jnp.float32),
            jax.ShapeDtypeStruct((feats, 1), jnp.float32),
        ]
        scratch += [
            pltpu.VMEM((heads, enc, block), jnp.float32),
            pltpu.VMEM((heads, enc, 2 * HEAD), jnp.float32),
        ]
    smem = pl.BlockSpec(memory_space=pltpu.SMEM)
    vmem = pl.BlockSpec(memory_space=pltpu.VMEM)
    return pl.pallas_call(
        functools.partial(attention_kernel, backward, active, width),
        out_shape=shapes,
        in_specs=[smem, smem] + [vmem] * (len(operands) - 2),
        out_specs=[vmem] * len(shapes),
        scratch_shapes=scratch,
        compiler_params=pltpu.CompilerParams(vmem_limit_bytes=VMEM_BYTES),
        cost_estimate=pl.CostEstimate(
            flops=(12 if backward else 4) * rows * enc * feats, bytes_accessed=4 * kv.size, transcendentals=rows * enc
        ),
        name="section_back" if backward else "section_ahead",
    )(*operands)


def totals_kernel(n, part_ref, total_ref, held, send_sem, recv_sem):
    me = lax.axis_index("seq")
    barrier = pltpu.get_barrier_semaphore()

    def greet(k, _):
        pl.semaphore_signal(barrier, inc=1, device_id={"seq": lax.rem(me + k, n)}, device_id_type=MESH)
        return 0

    lax.fori_loop(1, n, greet, 0)
    pl.semaphore_wait(barrier, n - 1)

    def copy(k, slot):
        return pltpu.make_async_remote_copy(
            src_ref=part_ref, dst_ref=held.at[slot], send_sem=send_sem.at[k], recv_sem=recv_sem.at[slot],
            device_id={"seq": lax.rem(me + k, n)}, device_id_type=MESH,
        )

    def send(k, _):
        copy(k, me).start()
        return 0

    lax.fori_loop(1, n, send, 0)

    def take(k, total):
        source = lax.rem(me + k, n)
        copy(k, source).wait_recv()
        return total + held[source]

    total_ref[...] = lax.fori_loop(1, n, take, part_ref[...])

    def finish(k, _):
        copy(k, me).wait_send()
        return 0

    lax.fori_loop(1, n, finish, 0)


def totals(n, part):
    vmem = pl.BlockSpec(memory_space=pltpu.VMEM)
    return pl.pallas_call(
        functools.partial(totals_kernel, n),
        out_shape=jax.ShapeDtypeStruct(part.shape, jnp.float32),
        in_specs=[vmem],
        out_specs=vmem,
        scratch_shapes=[
            pltpu.VMEM((n,) + part.shape, jnp.float32),
            pltpu.SemaphoreType.DMA((n,)),
            pltpu.SemaphoreType.DMA((n,)),
        ],
        compiler_params=pltpu.CompilerParams(collective_id=0, has_side_effects=True),
        name="row_totals",
    )(part)


def ahead_kernel(n, y_ref, x_ref, total_ref, part, held, send_sem, recv_sem, y_send, y_recv):
    me = lax.axis_index("seq")
    phase = lax.axis_index("phase")
    barrier = pltpu.get_barrier_semaphore()
    y_copy = pltpu.make_async_remote_copy(
        src_ref=y_ref, dst_ref=x_ref, send_sem=y_send, recv_sem=y_recv,
        device_id={"phase": 1 - phase, "seq": me}, device_id_type=MESH,
    )

    def copy(k, slot):
        return pltpu.make_async_remote_copy(
            src_ref=part, dst_ref=held.at[slot], send_sem=send_sem.at[k], recv_sem=recv_sem.at[slot],
            device_id={"phase": 1 - phase, "seq": lax.rem(me + k, n)}, device_id_type=MESH,
        )

    @pl.when(phase == 1)
    def _():
        def greet(k, _):
            pl.semaphore_signal(
                barrier, inc=1, device_id={"phase": 0, "seq": lax.rem(me + k, n)}, device_id_type=MESH
            )
            return 0

        lax.fori_loop(0, n, greet, 0)

        def take(k, total):
            source = lax.rem(me + k, n)
            copy(k, source).wait_recv()
            return total + held[source]

        total_ref[...] = lax.fori_loop(0, n, take, jnp.zeros(total_ref.shape, jnp.float32))
        y_copy.wait_recv()

    @pl.when(phase == 0)
    def _():
        yf = y_ref[...].astype(jnp.float32)
        part[...] = jnp.sum(yf * yf, axis=0, keepdims=True)
        pl.semaphore_wait(barrier, n)
        y_copy.start()

        def send(k, _):
            copy(k, me).start()
            return 0

        lax.fori_loop(0, n, send, 0)

        def finish(k, _):
            copy(k, me).wait_send()
            return 0

        lax.fori_loop(0, n, finish, 0)
        y_copy.wait_send()


def ahead(n, y):
    vmem = pl.BlockSpec(memory_space=pltpu.VMEM)
    rows = y.shape[1]
    return pl.pallas_call(
        functools.partial(ahead_kernel, n),
        out_shape=[jax.ShapeDtypeStruct(y.shape, y.dtype), jax.ShapeDtypeStruct((1, rows), jnp.float32)],
        in_specs=[vmem],
        out_specs=[vmem, vmem],
        scratch_shapes=[
            pltpu.VMEM((1, rows), jnp.float32),
            pltpu.VMEM((n, 1, rows), jnp.float32),
            pltpu.SemaphoreType.DMA((n,)),
            pltpu.SemaphoreType.DMA((n,)),
            pltpu.SemaphoreType.DMA,
            pltpu.SemaphoreType.DMA,
        ],
        compiler_params=pltpu.CompilerParams(collective_id=1, has_side_effects=True),
        name="relay_ahead",
    )(y)


def back_kernel(n, width, part_ref, cross_ref, x_ref, total_ref, g_ref, held, grad, send_sem, recv_sem, g_send, g_recv):
    me = lax.axis_index("seq")
    phase = lax.axis_index("phase")
    barrier = pltpu.get_barrier_semaphore()
    g_copy = pltpu.make_async_remote_copy(
        src_ref=grad, dst_ref=g_ref, send_sem=g_send, recv_sem=g_recv,
        device_id={"phase": 1 - phase, "seq": me}, device_id_type=MESH,
    )

    def copy(k, slot):
        return pltpu.make_async_remote_copy(
            src_ref=cross_ref, dst_ref=held.at[slot], send_sem=send_sem.at[k], recv_sem=recv_sem.at[slot],
            device_id={"phase": phase, "seq": lax.rem(me + k, n)}, device_id_type=MESH,
        )

    @pl.when(phase == 0)
    def _():
        pl.semaphore_signal(barrier, inc=1, device_id={"phase": 1, "seq": me}, device_id_type=MESH)
        g_copy.wait_recv()

    @pl.when(phase == 1)
    def _():
        def greet(k, _):
            pl.semaphore_signal(
                barrier, inc=1, device_id={"phase": 1, "seq": lax.rem(me + k, n)}, device_id_type=MESH
            )
            return 0

        lax.fori_loop(1, n, greet, 0)
        pl.semaphore_wait(barrier, n)

        def send(k, _):
            copy(k, me).start()
            return 0

        lax.fori_loop(1, n, send, 0)

        def take(k, total):
            source = lax.rem(me + k, n)
            copy(k, source).wait_recv()
            return total + held[source]

        cross = lax.fori_loop(1, n, take, cross_ref[...])
        inv = lax.rsqrt(total_ref[...] / width + eps)
        factor = inv * inv * inv * (cross / width)
        grad[...] = (part_ref[...] - x_ref[...].astype(jnp.float32) * factor).astype(jnp.bfloat16)
        g_copy.start()

        def finish(k, _):
            copy(k, me).wait_send()
            return 0

        lax.fori_loop(1, n, finish, 0)
        g_copy.wait_send()


def back(n, width, part, cross, x, total):
    vmem = pl.BlockSpec(memory_space=pltpu.VMEM)
    rows = x.shape[1]
    return pl.pallas_call(
        functools.partial(back_kernel, n, width),
        out_shape=jax.ShapeDtypeStruct(x.shape, jnp.bfloat16),
        in_specs=[vmem] * 4,
        out_specs=vmem,
        scratch_shapes=[
            pltpu.VMEM((n, 1, rows), jnp.float32),
            pltpu.VMEM(x.shape, jnp.bfloat16),
            pltpu.SemaphoreType.DMA((n,)),
            pltpu.SemaphoreType.DMA((n,)),
            pltpu.SemaphoreType.DMA,
            pltpu.SemaphoreType.DMA,
        ],
        compiler_params=pltpu.CompilerParams(collective_id=2, has_side_effects=True),
        name="relay_back",
    )(part, cross, x, total)


def doc_bounds(qseg, kseg):
    block = min(QROWS, qseg.shape[0])
    chunk = min(CHUNK, kseg.shape[0])
    blocks = qseg.reshape(-1, block)
    below = jnp.sum(kseg[None, :] < blocks[:, :1], axis=1)
    upto = jnp.sum(kseg[None, :] <= blocks[:, -1:], axis=1)
    return jnp.stack([below // chunk, (upto + chunk - 1) // chunk], axis=1).reshape(-1).astype(jnp.int32)


def local(n, dec_in, enc_kv, dec_seg, enc_seg, q_gain, o_gain, cotangent):
    phase = lax.axis_index("phase")
    micro, rows, feats = dec_in.shape
    own_enc = enc_kv.shape[2]
    enc = enc_seg.shape[1]
    width = feats * n
    flag = phase.astype(jnp.int32).reshape(1)
    qg = q_gain.reshape(feats, 1)
    og = o_gain.reshape(feats, 1)
    inputs = dec_in.transpose(0, 2, 1)
    wanted = cotangent.transpose(0, 2, 1)
    xf = inputs.astype(jnp.float32)
    first_totals = totals(n, jnp.sum(xf * xf, axis=1))
    scattered = []
    for m in range(micro):
        blocks = enc_kv[0, m].reshape(own_enc, n, 2 * feats).transpose(1, 0, 2)
        if m > 0:
            blocks, scattered[-1], first_totals = lax.optimization_barrier((blocks, scattered[-1], first_totals))
        scattered.append(lax.all_to_all(blocks, "seq", split_axis=0, concat_axis=0, tiled=True))

    calls, x0s, t0s = [], [], []
    for m in range(micro):
        calls.append(functools.partial(
            attention, width=width, phase=flag, bounds=doc_bounds(dec_seg[m], enc_seg[m]),
            kv=scattered[m].reshape(enc, 2 * feats), kseg=enc_seg[m].reshape(enc, 1),
            qseg=dec_seg[m].reshape(1, rows), qg=qg, og=og,
        ))
        x0s.append(inputs[m])
        t0s.append(first_totals[m].reshape(1, rows))
    outs, grads, gqgs, gogs = [], [], [], []

    def finish(m, y0, first, g0):
        y1, gkv1, gqg1, gog1 = first
        _, gkv0, _, _, gqg0, gog0 = calls[m](True, 0, x=x0s[m], total=t0s[m], g=g0)
        outs.append(jnp.where(phase == 0, y0, y1).T)
        grads.append(jnp.where(phase == 0, gkv0, gkv1).reshape(n, own_enc, 2 * feats))
        gqgs.append(jnp.where(phase == 0, gqg0, gqg1))
        gogs.append(jnp.where(phase == 0, gog0, gog1))

    y0 = calls[0](False, 0, x=x0s[0], total=t0s[0])[0]
    waiting = None
    for m in range(micro):
        x1, total1 = ahead(n, y0)
        if waiting is not None:
            x1, waiting[2] = lax.optimization_barrier((x1, waiting[2]))
        y1, gkv1, part, cross, gqg1, gog1 = calls[m](True, 1, x=x1, total=total1, g=wanted[m])
        if waiting is not None:
            waiting[2], part = lax.optimization_barrier((waiting[2], part))
            finish(m - 1, *waiting)
        later = None
        if m + 1 < micro:
            x_next, part = lax.optimization_barrier((x0s[m + 1], part))
            later = calls[m + 1](False, 0, x=x_next, total=t0s[m + 1])[0]
            cross, later = lax.optimization_barrier((cross, later))
        g0 = back(n, width, part, cross, x1, total1)
        if grads:
            grads[-1], g0 = lax.optimization_barrier((grads[-1], g0))
        if later is not None:
            later, g0 = lax.optimization_barrier((later, g0))
        waiting = [y0, (y1, gkv1, gqg1, gog1), g0]
        y0 = later
    finish(micro - 1, *waiting)
    returned = []
    for m in range(micro):
        rows_back = lax.all_to_all(grads[m], "seq", split_axis=0, concat_axis=0, tiled=True)
        returned.append(rows_back.transpose(1, 0, 2).reshape(own_enc, 2 * feats * n))
    return (
        jnp.stack(outs)[None],
        jnp.stack(returned)[None],
        sum(gqgs).reshape(1, feats),
        sum(gogs).reshape(1, feats),
    )


def solution(mesh):
    in_specs = (
        P(None, None, "seq"),
        P("phase", None, "seq", None),
        P(),
        P(),
        P("phase", "seq"),
        P("phase", "seq"),
        P(None, None, "seq"),
    )
    out_specs = (
        P("phase", None, None, "seq"),
        P("phase", None, "seq", None),
        P("phase", "seq"),
        P("phase", "seq"),
    )
    body = functools.partial(local, mesh.shape["seq"])
    return jax.shard_map(body, mesh=mesh, in_specs=in_specs, out_specs=out_specs, check_vma=False)
```

```python
import functools

import jax
import jax.numpy as jnp
from jax import lax
from jax.experimental import pallas as pl
from jax.experimental.pallas import tpu as pltpu
from jax.sharding import PartitionSpec as P

HEAD = 64
QROWS = 256
CHUNK = 256
SCALE = 0.125

eps = 1e-06
neg_big = -1e30
MESH = pl.DeviceIdType.MESH
VMEM_BYTES = 36 * 1024 * 1024


def matmul(a, b):
    return lax.dot_general(a, b, (((1,), (0,)), ((), ())), preferred_element_type=jnp.float32)


def matmul_t(a, b):
    return lax.dot_general(a, b, (((1,), (1,)), ((), ())), preferred_element_type=jnp.float32)


def attention_kernel(backward, active, width, *refs):
    if backward:
        (phase_ref, bound_ref, kv_ref, kseg_ref, qseg_ref, x_ref, total_ref, qg_ref, og_ref, g_ref,
         y_ref, gkv_ref, part_ref, cross_ref, gqg_ref, gog_ref,
         score_ref, top_ref, kvt_ref, pair_ref, gprob_ref, acc_ref) = refs
    else:
        (phase_ref, bound_ref, kv_ref, kseg_ref, qseg_ref, x_ref, total_ref, qg_ref, og_ref,
         y_ref, score_ref, top_ref, kvt_ref, pair_ref) = refs
    enc = kv_ref.shape[0]
    feats, rows = x_ref.shape
    heads = feats // HEAD
    block = min(QROWS, rows)
    chunk = min(CHUNK, enc)
    every = range(heads)
    lanes = [slice(2 * HEAD * h, 2 * HEAD * (h + 1)) for h in every]
    owns = [slice(HEAD * h, HEAD * (h + 1)) for h in every]

    def place(c):
        return pl.ds(pl.multiple_of(c * chunk, chunk), chunk)

    def work():
        def turn(c, _):
            at = place(c)
            for h in every:
                kvt_ref[h, :, at] = kv_ref[at, lanes[h]].T
                if backward:
                    acc_ref[h, at, :] = jnp.zeros((chunk, 2 * HEAD), jnp.float32)
            return 0

        lax.fori_loop(0, enc // chunk, turn, 0)
        row = jnp.zeros((1, block), jnp.float32)
        tall = jnp.zeros((2 * HEAD, block), jnp.float32)
        blank = jnp.zeros((HEAD, block), jnp.bfloat16)
        for b in range(rows // block):
            cols = slice(b * block, (b + 1) * block)
            low = bound_ref[2 * b]
            high = bound_ref[2 * b + 1]
            inv = lax.rsqrt(total_ref[:, cols] / width + eps)
            qseg = qseg_ref[:, cols]

            def normed_of(h):
                return x_ref[owns[h], cols].astype(jnp.float32) * inv

            for h in every:
                query = (normed_of(h) * qg_ref[owns[h], :]).astype(jnp.bfloat16)
                scaled = (query.astype(jnp.float32) * SCALE).astype(jnp.bfloat16)
                pair_ref[h, :, :block] = jnp.concatenate([scaled, blank], axis=0)
                if backward:
                    grad = (g_ref[owns[h], cols].astype(jnp.float32) * og_ref[owns[h], :]).astype(jnp.bfloat16)
                    pair_ref[h, :, block:] = jnp.concatenate([blank, grad], axis=0)

            def scores(c, carry):
                at = place(c)
                allowed = kseg_ref[at, :] == qseg
                found = []
                for h in every:
                    top, total = carry[h]
                    s = matmul(kv_ref[at, lanes[h]], pair_ref[h, :, :block])
                    s = jnp.where(allowed, s, neg_big)
                    higher = jnp.maximum(top, jnp.max(s, axis=0, keepdims=True))
                    e = jnp.exp(s - higher)
                    score_ref[h, at, :] = e
                    top_ref[h, pl.ds(c, 1), :] = higher
                    found.append((higher, total * jnp.exp(top - higher) + jnp.sum(e, axis=0, keepdims=True)))
                return tuple(found)

            found = lax.fori_loop(low, high, scores, tuple((row + neg_big, row) for h in every))
            tops = [top for top, _ in found]
            shares = [1.0 / total for _, total in found]

            def probs_of(h, c, at):
                return score_ref[h, at, :] * (jnp.exp(top_ref[h, pl.ds(c, 1), :] - tops[h]) * shares[h])

            if not backward:
                def outputs(c, outs):
                    at = place(c)
                    return tuple(
                        outs[h] + matmul(kvt_ref[h, :, at], probs_of(h, c, at).astype(jnp.bfloat16)) for h in every
                    )

                outs = lax.fori_loop(low, high, outputs, tuple(tall for h in every))
                for h in every:
                    xf = x_ref[owns[h], cols].astype(jnp.float32)
                    y_ref[owns[h], cols] = (xf + og_ref[owns[h], :] * outs[h][HEAD:]).astype(jnp.bfloat16)
                continue

            def outputs_and_delta(c, carry):
                at = place(c)
                found = []
                for h in every:
                    out, delta = carry[h]
                    probs = probs_of(h, c, at)
                    score_ref[h, at, :] = probs
                    gprob = matmul(kv_ref[at, lanes[h]], pair_ref[h, :, block:])
                    gprob_ref[h, at, :] = gprob
                    out = out + matmul(kvt_ref[h, :, at], probs.astype(jnp.bfloat16))
                    found.append((out, delta + jnp.sum(probs * gprob, axis=0, keepdims=True)))
                return tuple(found)

            found = lax.fori_loop(low, high, outputs_and_delta, tuple((tall, row) for h in every))
            outs = [out for out, _ in found]
            deltas = [delta for _, delta in found]

            def gradients(c, gqs):
                at = place(c)
                found = []
                for h in every:
                    probs = score_ref[h, at, :]
                    gscore = (probs * (gprob_ref[h, at, :] - deltas[h])).astype(jnp.bfloat16)
                    both = jnp.concatenate([gscore, probs.astype(jnp.bfloat16)], axis=1)
                    acc_ref[h, at, :] += matmul_t(both, pair_ref[h])
                    found.append(gqs[h] + matmul(kvt_ref[h, :, at], gscore))
                return tuple(found)

            gqs = lax.fori_loop(low, high, gradients, tuple(tall for h in every))
            cross = row
            for h in every:
                own = owns[h]
                xf = x_ref[own, cols].astype(jnp.float32)
                gf = g_ref[own, cols].astype(jnp.float32)
                out = outs[h][HEAD:]
                gq = gqs[h][:HEAD] * SCALE
                gn = gq * qg_ref[own, :]
                y_ref[own, cols] = (xf + og_ref[own, :] * out).astype(jnp.bfloat16)
                part_ref[own, cols] = gf + inv * gn
                cross = cross + jnp.sum(gn * xf, axis=0, keepdims=True)
                gqg = jnp.sum(gq * normed_of(h), axis=1, keepdims=True)
                gog = jnp.sum(gf * out, axis=1, keepdims=True)
                gqg_ref[own, :] = gqg if b == 0 else gqg_ref[own, :] + gqg
                gog_ref[own, :] = gog if b == 0 else gog_ref[own, :] + gog
            cross_ref[:, cols] = cross
        if backward:
            def store(c, _):
                at = place(c)
                for h in every:
                    gkv_ref[at, lanes[h]] = acc_ref[h, at, :].astype(jnp.bfloat16)
                return 0

            lax.fori_loop(0, enc // chunk, store, 0)

    pl.when(phase_ref[0] == active)(work)


def attention(backward, active, width, phase, bounds, kv, kseg, qseg, x, total, qg, og, g=None):
    enc = kv.shape[0]
    feats, rows = x.shape
    block = min(QROWS, rows)
    shapes = [jax.ShapeDtypeStruct((feats, rows), jnp.bfloat16)]
    heads = feats // HEAD
    scratch = [
        pltpu.VMEM((heads, enc, block), jnp.float32),
        pltpu.VMEM((heads, max(8, enc // min(CHUNK, enc)), block), jnp.float32),
        pltpu.VMEM((heads, 2 * HEAD, enc), jnp.bfloat16),
        pltpu.VMEM((heads, 2 * HEAD, 2 * block if backward else block), jnp.bfloat16),
    ]
    operands = [phase, bounds, kv, kseg, qseg, x, total, qg, og]
    if backward:
        operands.append(g)
        shapes += [
            jax.ShapeDtypeStruct(kv.shape, jnp.bfloat16),
            jax.ShapeDtypeStruct((feats, rows), jnp.float32),
            jax.ShapeDtypeStruct((1, rows), jnp.float32),
            jax.ShapeDtypeStruct((feats, 1), jnp.float32),
            jax.ShapeDtypeStruct((feats, 1), jnp.float32),
        ]
        scratch += [
            pltpu.VMEM((heads, enc, block), jnp.float32),
            pltpu.VMEM((heads, enc, 2 * HEAD), jnp.float32),
        ]
    smem = pl.BlockSpec(memory_space=pltpu.SMEM)
    vmem = pl.BlockSpec(memory_space=pltpu.VMEM)
    return pl.pallas_call(
        functools.partial(attention_kernel, backward, active, width),
        out_shape=shapes,
        in_specs=[smem, smem] + [vmem] * (len(operands) - 2),
        out_specs=[vmem] * len(shapes),
        scratch_shapes=scratch,
        compiler_params=pltpu.CompilerParams(vmem_limit_bytes=VMEM_BYTES),
        cost_estimate=pl.CostEstimate(
            flops=(72 if backward else 32) * rows * enc * feats, bytes_accessed=4 * kv.size,
            transcendentals=rows * enc * heads,
        ),
        name="section_back" if backward else "section_ahead",
    )(*operands)


def totals_kernel(n, part_ref, total_ref, held, send_sem, recv_sem):
    me = lax.axis_index("seq")
    barrier = pltpu.get_barrier_semaphore()

    def greet(k, _):
        pl.semaphore_signal(barrier, inc=1, device_id={"seq": lax.rem(me + k, n)}, device_id_type=MESH)
        return 0

    lax.fori_loop(1, n, greet, 0)
    pl.semaphore_wait(barrier, n - 1)

    def copy(k, slot):
        return pltpu.make_async_remote_copy(
            src_ref=part_ref, dst_ref=held.at[slot], send_sem=send_sem.at[k], recv_sem=recv_sem.at[slot],
            device_id={"seq": lax.rem(me + k, n)}, device_id_type=MESH,
        )

    def send(k, _):
        copy(k, me).start()
        return 0

    lax.fori_loop(1, n, send, 0)

    def take(k, total):
        source = lax.rem(me + k, n)
        copy(k, source).wait_recv()
        return total + held[source]

    total_ref[...] = lax.fori_loop(1, n, take, part_ref[...])

    def finish(k, _):
        copy(k, me).wait_send()
        return 0

    lax.fori_loop(1, n, finish, 0)


def totals(n, part):
    vmem = pl.BlockSpec(memory_space=pltpu.VMEM)
    return pl.pallas_call(
        functools.partial(totals_kernel, n),
        out_shape=jax.ShapeDtypeStruct(part.shape, jnp.float32),
        in_specs=[vmem],
        out_specs=vmem,
        scratch_shapes=[
            pltpu.VMEM((n,) + part.shape, jnp.float32),
            pltpu.SemaphoreType.DMA((n,)),
            pltpu.SemaphoreType.DMA((n,)),
        ],
        compiler_params=pltpu.CompilerParams(collective_id=0, has_side_effects=True),
        name="row_totals",
    )(part)


def exchange_kernel(n, width, ahead, back, *refs):
    refs = list(refs)
    y_ref = refs.pop(0) if ahead else None
    part_ref, cross_ref, x_ref, total_ref = [refs.pop(0) for _ in range(4)] if back else [None] * 4
    x_out, total_out = [refs.pop(0) for _ in range(2)] if ahead else [None] * 2
    g_out = refs.pop(0) if back else None
    if ahead:
        square, held, send_sem, recv_sem, y_send, y_recv = [refs.pop(0) for _ in range(6)]
    if back:
        crosses, grad, cross_send, cross_recv, g_send, g_recv = [refs.pop(0) for _ in range(6)]
    me = lax.axis_index("seq")
    phase = lax.axis_index("phase")
    barrier = pltpu.get_barrier_semaphore()

    def other(k):
        return lax.rem(me + k, n)

    def greet(section, start):
        def signal(k, _):
            pl.semaphore_signal(
                barrier, inc=1, device_id={"phase": section, "seq": other(k)}, device_id_type=MESH
            )
            return 0

        lax.fori_loop(start, n, signal, 0)

    if ahead:
        y_copy = pltpu.make_async_remote_copy(
            src_ref=y_ref, dst_ref=x_out, send_sem=y_send, recv_sem=y_recv,
            device_id={"phase": 1 - phase, "seq": me}, device_id_type=MESH,
        )

        def square_copy(k, slot):
            return pltpu.make_async_remote_copy(
                src_ref=square, dst_ref=held.at[slot], send_sem=send_sem.at[k], recv_sem=recv_sem.at[slot],
                device_id={"phase": 1 - phase, "seq": other(k)}, device_id_type=MESH,
            )

    if back:
        g_copy = pltpu.make_async_remote_copy(
            src_ref=grad, dst_ref=g_out, send_sem=g_send, recv_sem=g_recv,
            device_id={"phase": 1 - phase, "seq": me}, device_id_type=MESH,
        )

        def cross_copy(k, slot):
            return pltpu.make_async_remote_copy(
                src_ref=cross_ref, dst_ref=crosses.at[slot], send_sem=cross_send.at[k],
                recv_sem=cross_recv.at[slot],
                device_id={"phase": phase, "seq": other(k)}, device_id_type=MESH,
            )

    @pl.when(phase == 1)
    def _():
        if back:
            greet(1, 1)
        if ahead:
            greet(0, 0)
        if back:
            pl.semaphore_wait(barrier, n)

            def send(k, _):
                cross_copy(k, me).start()
                return 0

            lax.fori_loop(1, n, send, 0)

            def take(k, total):
                cross_copy(k, other(k)).wait_recv()
                return total + crosses[other(k)]

            cross = lax.fori_loop(1, n, take, cross_ref[...])
            inv = lax.rsqrt(total_ref[...] / width + eps)
            factor = inv * inv * inv * (cross / width)
            grad[...] = (part_ref[...] - x_ref[...].astype(jnp.float32) * factor).astype(jnp.bfloat16)
            g_copy.start()
        if ahead:
            def take_square(k, total):
                square_copy(k, other(k)).wait_recv()
                return total + held[other(k)]

            total_out[...] = lax.fori_loop(0, n, take_square, jnp.zeros(total_out.shape, jnp.float32))
            y_copy.wait_recv()
        if back:
            def finish(k, _):
                cross_copy(k, me).wait_send()
                return 0

            lax.fori_loop(1, n, finish, 0)
            g_copy.wait_send()

    @pl.when(phase == 0)
    def _():
        if back:
            pl.semaphore_signal(barrier, inc=1, device_id={"phase": 1, "seq": me}, device_id_type=MESH)
        if ahead:
            yf = y_ref[...].astype(jnp.float32)
            square[...] = jnp.sum(yf * yf, axis=0, keepdims=True)
            pl.semaphore_wait(barrier, n)

            def send(k, _):
                square_copy(k, me).start()
                return 0

            lax.fori_loop(0, n, send, 0)
            y_copy.start()
        if back:
            g_copy.wait_recv()
        if ahead:
            def finish(k, _):
                square_copy(k, me).wait_send()
                return 0

            lax.fori_loop(0, n, finish, 0)
            y_copy.wait_send()


def exchange(n, width, y=None, back=None):
    vmem = pl.BlockSpec(memory_space=pltpu.VMEM)
    ahead = y is not None
    operands, shapes, scratch = [], [], []
    feats, rows = y.shape if ahead else back[0].shape
    whole = jax.ShapeDtypeStruct((feats, rows), jnp.bfloat16)
    row = jax.ShapeDtypeStruct((1, rows), jnp.float32)
    sems = [pltpu.SemaphoreType.DMA((n,)), pltpu.SemaphoreType.DMA((n,)), pltpu.SemaphoreType.DMA, pltpu.SemaphoreType.DMA]
    if ahead:
        operands.append(y)
        shapes += [whole, row]
        scratch += [pltpu.VMEM((1, rows), jnp.float32), pltpu.VMEM((n, 1, rows), jnp.float32)] + sems
    if back is not None:
        operands += list(back)
        shapes.append(whole)
        scratch += [pltpu.VMEM((n, 1, rows), jnp.float32), pltpu.VMEM((feats, rows), jnp.bfloat16)] + sems
    return pl.pallas_call(
        functools.partial(exchange_kernel, n, width, ahead, back is not None),
        out_shape=shapes,
        in_specs=[vmem] * len(operands),
        out_specs=[vmem] * len(shapes),
        scratch_shapes=scratch,
        compiler_params=pltpu.CompilerParams(
            collective_id=int(ahead) + 2 * int(back is not None), has_side_effects=True
        ),
        name="exchange" + ("_ahead" if ahead else "") + ("_back" if back is not None else ""),
    )(*operands)


def scatter_kernel(m, kv_ref, out_ref, sems):
    n, _, columns = out_ref.shape
    copies = [
        pltpu.make_async_copy(kv_ref.at[0, m, :, pl.ds(j * columns, columns)], out_ref.at[j], sems.at[j])
        for j in range(n)
    ]
    for copy in copies:
        copy.start()
    for copy in copies:
        copy.wait()


def scatter(n, m, enc_kv):
    _, _, rows, columns = enc_kv.shape
    spec = pl.BlockSpec(memory_space=pl.ANY)
    return pl.pallas_call(
        functools.partial(scatter_kernel, m),
        out_shape=jax.ShapeDtypeStruct((n, rows, columns // n), enc_kv.dtype),
        in_specs=[spec],
        out_specs=spec,
        scratch_shapes=[pltpu.SemaphoreType.DMA((n,))],
        name="scatter",
    )(enc_kv)


def gather_kernel(*refs):
    *parts, out_ref, sems = refs
    n, _, columns = parts[0].shape
    copies = [
        pltpu.make_async_copy(part.at[j], out_ref.at[0, m, :, pl.ds(j * columns, columns)], sems.at[m * n + j])
        for m, part in enumerate(parts) for j in range(n)
    ]
    for copy in copies:
        copy.start()
    for copy in copies:
        copy.wait()


def gather(parts):
    n, rows, columns = parts[0].shape
    spec = pl.BlockSpec(memory_space=pl.ANY)
    return pl.pallas_call(
        gather_kernel,
        out_shape=jax.ShapeDtypeStruct((1, len(parts), rows, n * columns), parts[0].dtype),
        in_specs=[spec] * len(parts),
        out_specs=spec,
        scratch_shapes=[pltpu.SemaphoreType.DMA((n * len(parts),))],
        name="gather",
    )(*parts)


def doc_bounds(qseg, kseg):
    block = min(QROWS, qseg.shape[0])
    chunk = min(CHUNK, kseg.shape[0])
    blocks = qseg.reshape(-1, block)
    below = jnp.sum(kseg[None, :] < blocks[:, :1], axis=1)
    upto = jnp.sum(kseg[None, :] <= blocks[:, -1:], axis=1)
    return jnp.stack([below // chunk, (upto + chunk - 1) // chunk], axis=1).reshape(-1).astype(jnp.int32)


def local(n, dec_in, enc_kv, dec_seg, enc_seg, q_gain, o_gain, cotangent):
    phase = lax.axis_index("phase")
    micro, rows, feats = dec_in.shape
    own_enc = enc_kv.shape[2]
    enc = enc_seg.shape[1]
    width = feats * n
    flag = phase.astype(jnp.int32).reshape(1)
    qg = q_gain.reshape(feats, 1)
    og = o_gain.reshape(feats, 1)
    inputs = dec_in.transpose(0, 2, 1)
    wanted = cotangent.transpose(0, 2, 1)
    xf = inputs.astype(jnp.float32)
    first_totals = totals(n, jnp.sum(xf * xf, axis=1))
    scattered = []
    for m in range(micro):
        blocks = scatter(n, m, enc_kv)
        if m > 0:
            blocks, scattered[-1] = lax.optimization_barrier((blocks, scattered[-1]))
        else:
            blocks, first_totals = lax.optimization_barrier((blocks, first_totals))
        scattered.append(lax.all_to_all(blocks, "seq", split_axis=0, concat_axis=0, tiled=True))

    calls, x0s, t0s = [], [], []
    for m in range(micro):
        calls.append(functools.partial(
            attention, width=width, phase=flag, bounds=doc_bounds(dec_seg[m], enc_seg[m]),
            kv=scattered[m].reshape(enc, 2 * feats), kseg=enc_seg[m].reshape(enc, 1),
            qseg=dec_seg[m].reshape(1, rows), qg=qg, og=og,
        ))
        x0s.append(inputs[m])
        t0s.append(first_totals[m].reshape(1, rows))
    outs, grads, gqgs, gogs = [], [], [], []

    def finish(m, y0, first, g0):
        y1, gkv1, gqg1, gog1 = first
        _, gkv0, _, _, gqg0, gog0 = calls[m](True, 0, x=x0s[m], total=t0s[m], g=g0)
        outs.append(jnp.where(phase == 0, y0, y1).T)
        grads.append(jnp.where(phase == 0, gkv0, gkv1).reshape(n, own_enc, 2 * feats))
        gqgs.append(jnp.where(phase == 0, gqg0, gqg1))
        gogs.append(jnp.where(phase == 0, gog0, gog1))

    y0 = calls[0](False, 0, x=x0s[0], total=t0s[0])[0]
    x1, total1 = exchange(n, width, y=y0)
    waiting = None
    for m in range(micro):
        y1, gkv1, part, cross, gqg1, gog1 = calls[m](True, 1, x=x1, total=total1, g=wanted[m])
        if waiting is not None:
            waiting[2], part = lax.optimization_barrier((waiting[2], part))
            finish(m - 1, *waiting)
        waiting = [y0, (y1, gkv1, gqg1, gog1), None]
        if m + 1 < micro:
            x_next, part = lax.optimization_barrier((x0s[m + 1], part))
            y0 = calls[m + 1](False, 0, x=x_next, total=t0s[m + 1])[0]
            x1, total1, waiting[2] = exchange(n, width, y=y0, back=(part, cross, x1, total1))
        else:
            waiting[2] = exchange(n, width, back=(part, cross, x1, total1))[0]
            if grads:
                grads[-1], waiting[2] = lax.optimization_barrier((grads[-1], waiting[2]))
    finish(micro - 1, *waiting)
    returned = []
    for m in range(micro):
        returned.append(lax.all_to_all(grads[m], "seq", split_axis=0, concat_axis=0, tiled=True))
    return (
        jnp.stack(outs)[None],
        gather(returned),
        sum(gqgs).reshape(1, feats),
        sum(gogs).reshape(1, feats),
    )


def solution(mesh):
    in_specs = (
        P(None, None, "seq"),
        P("phase", None, "seq", None),
        P(),
        P(),
        P("phase", "seq"),
        P("phase", "seq"),
        P(None, None, "seq"),
    )
    out_specs = (
        P("phase", None, None, "seq"),
        P("phase", None, "seq", None),
        P("phase", "seq"),
        P("phase", "seq"),
    )
    body = functools.partial(local, mesh.shape["seq"])
    return jax.shard_map(body, mesh=mesh, in_specs=in_specs, out_specs=out_specs, check_vma=False)
```

```python
import functools

import jax
import jax.numpy as jnp
from jax import lax
from jax.experimental import pallas as pl
from jax.experimental.pallas import tpu as pltpu
from jax.sharding import PartitionSpec as P

HEAD = 64
QROWS = 256
CHUNK = 256
SCALE = 0.125

eps = 1e-06
neg_big = -1e30
MESH = pl.DeviceIdType.MESH
VMEM_BYTES = 56 * 1024 * 1024


def matmul(a, b):
    return lax.dot_general(a, b, (((1,), (0,)), ((), ())), preferred_element_type=jnp.float32)


def matmul_t(a, b):
    return lax.dot_general(a, b, (((1,), (1,)), ((), ())), preferred_element_type=jnp.float32)


def attention_kernel(backward, active, width, *refs):
    if backward:
        (phase_ref, bound_ref, kv_ref, kseg_ref, qseg_ref, x_ref, total_ref, qg_ref, og_ref, g_ref,
         y_ref, gkv_ref, part_ref, cross_ref, gqg_ref, gog_ref,
         score_ref, top_ref, kvt_ref, pair_ref, gprob_ref, acc_ref) = refs
    else:
        (phase_ref, bound_ref, kv_ref, kseg_ref, qseg_ref, x_ref, total_ref, qg_ref, og_ref,
         y_ref, score_ref, top_ref, kvt_ref, pair_ref) = refs
    enc = kv_ref.shape[0]
    feats, rows = x_ref.shape
    heads = feats // HEAD
    block = min(QROWS, rows)
    chunk = min(CHUNK, enc)
    every = range(heads)
    lanes = [slice(2 * HEAD * h, 2 * HEAD * (h + 1)) for h in every]
    owns = [slice(HEAD * h, HEAD * (h + 1)) for h in every]

    def place(c):
        return pl.ds(pl.multiple_of(c * chunk, chunk), chunk)

    def work():
        def turn(c, _):
            at = place(c)
            for h in every:
                kvt_ref[h, :, at] = kv_ref[at, lanes[h]].T
                if backward:
                    acc_ref[h, at, :] = jnp.zeros((chunk, 2 * HEAD), jnp.float32)
            return 0

        lax.fori_loop(0, enc // chunk, turn, 0)
        row = jnp.zeros((1, block), jnp.float32)
        tall = jnp.zeros((2 * HEAD, block), jnp.float32)
        blank = jnp.zeros((HEAD, block), jnp.bfloat16)
        for b in range(rows // block):
            cols = slice(b * block, (b + 1) * block)
            low = bound_ref[2 * b]
            high = bound_ref[2 * b + 1]
            inv = lax.rsqrt(total_ref[:, cols] / width + eps)
            qseg = qseg_ref[:, cols]

            def normed_of(h):
                return x_ref[owns[h], cols].astype(jnp.float32) * inv

            for h in every:
                query = (normed_of(h) * qg_ref[owns[h], :]).astype(jnp.bfloat16)
                scaled = (query.astype(jnp.float32) * SCALE).astype(jnp.bfloat16)
                pair_ref[h, :, :block] = jnp.concatenate([scaled, blank], axis=0)
                if backward:
                    grad = (g_ref[owns[h], cols].astype(jnp.float32) * og_ref[owns[h], :]).astype(jnp.bfloat16)
                    pair_ref[h, :, block:] = jnp.concatenate([blank, grad], axis=0)

            def scores(c, carry):
                at = place(c)
                allowed = kseg_ref[at, :] == qseg
                found = []
                for h in every:
                    top, total = carry[h]
                    s = matmul(kv_ref[at, lanes[h]], pair_ref[h, :, :block])
                    s = jnp.where(allowed, s, neg_big)
                    higher = jnp.maximum(top, jnp.max(s, axis=0, keepdims=True))
                    e = jnp.exp(s - higher)
                    score_ref[h, at, :] = e
                    top_ref[h, pl.ds(c, 1), :] = higher
                    found.append((higher, total * jnp.exp(top - higher) + jnp.sum(e, axis=0, keepdims=True)))
                return tuple(found)

            found = lax.fori_loop(low, high, scores, tuple((row + neg_big, row) for h in every))
            tops = [top for top, _ in found]
            shares = [1.0 / total for _, total in found]

            def probs_of(h, c, at):
                return score_ref[h, at, :] * (jnp.exp(top_ref[h, pl.ds(c, 1), :] - tops[h]) * shares[h])

            if not backward:
                def outputs(c, outs):
                    at = place(c)
                    return tuple(
                        outs[h] + matmul(kvt_ref[h, :, at], probs_of(h, c, at).astype(jnp.bfloat16)) for h in every
                    )

                outs = lax.fori_loop(low, high, outputs, tuple(tall for h in every))
                for h in every:
                    xf = x_ref[owns[h], cols].astype(jnp.float32)
                    y_ref[owns[h], cols] = (xf + og_ref[owns[h], :] * outs[h][HEAD:]).astype(jnp.bfloat16)
                continue

            def outputs_and_delta(c, carry):
                at = place(c)
                found = []
                for h in every:
                    out, delta = carry[h]
                    probs = probs_of(h, c, at)
                    score_ref[h, at, :] = probs
                    gprob = matmul(kv_ref[at, lanes[h]], pair_ref[h, :, block:])
                    gprob_ref[h, at, :] = gprob
                    out = out + matmul(kvt_ref[h, :, at], probs.astype(jnp.bfloat16))
                    found.append((out, delta + jnp.sum(probs * gprob, axis=0, keepdims=True)))
                return tuple(found)

            found = lax.fori_loop(low, high, outputs_and_delta, tuple((tall, row) for h in every))
            outs = [out for out, _ in found]
            deltas = [delta for _, delta in found]

            def gradients(c, gqs):
                at = place(c)
                found = []
                for h in every:
                    probs = score_ref[h, at, :]
                    gscore = (probs * (gprob_ref[h, at, :] - deltas[h])).astype(jnp.bfloat16)
                    both = jnp.concatenate([gscore, probs.astype(jnp.bfloat16)], axis=1)
                    acc_ref[h, at, :] += matmul_t(both, pair_ref[h])
                    found.append(gqs[h] + matmul(kvt_ref[h, :, at], gscore))
                return tuple(found)

            gqs = lax.fori_loop(low, high, gradients, tuple(tall for h in every))
            cross = row
            for h in every:
                own = owns[h]
                xf = x_ref[own, cols].astype(jnp.float32)
                gf = g_ref[own, cols].astype(jnp.float32)
                out = outs[h][HEAD:]
                gq = gqs[h][:HEAD] * SCALE
                gn = gq * qg_ref[own, :]
                y_ref[own, cols] = (xf + og_ref[own, :] * out).astype(jnp.bfloat16)
                part_ref[own, cols] = gf + inv * gn
                cross = cross + jnp.sum(gn * xf, axis=0, keepdims=True)
                gqg = jnp.sum(gq * normed_of(h), axis=1, keepdims=True)
                gog = jnp.sum(gf * out, axis=1, keepdims=True)
                gqg_ref[own, :] = gqg if b == 0 else gqg_ref[own, :] + gqg
                gog_ref[own, :] = gog if b == 0 else gog_ref[own, :] + gog
            cross_ref[:, cols] = cross
        if backward:
            def store(c, _):
                at = place(c)
                for h in every:
                    gkv_ref[at, lanes[h]] = acc_ref[h, at, :].astype(jnp.bfloat16)
                return 0

            lax.fori_loop(0, enc // chunk, store, 0)

    pl.when(phase_ref[0] == active)(work)


def attention(backward, active, width, phase, bounds, kv, kseg, qseg, x, total, qg, og, g=None):
    enc = kv.shape[0]
    feats, rows = x.shape
    block = min(QROWS, rows)
    shapes = [jax.ShapeDtypeStruct((feats, rows), jnp.bfloat16)]
    heads = feats // HEAD
    scratch = [
        pltpu.VMEM((heads, enc, block), jnp.float32),
        pltpu.VMEM((heads, max(8, enc // min(CHUNK, enc)), block), jnp.float32),
        pltpu.VMEM((heads, 2 * HEAD, enc), jnp.bfloat16),
        pltpu.VMEM((heads, 2 * HEAD, 2 * block if backward else block), jnp.bfloat16),
    ]
    operands = [phase, bounds, kv, kseg, qseg, x, total, qg, og]
    if backward:
        operands.append(g)
        shapes += [
            jax.ShapeDtypeStruct(kv.shape, jnp.bfloat16),
            jax.ShapeDtypeStruct((feats, rows), jnp.float32),
            jax.ShapeDtypeStruct((1, rows), jnp.float32),
            jax.ShapeDtypeStruct((feats, 1), jnp.float32),
            jax.ShapeDtypeStruct((feats, 1), jnp.float32),
        ]
        scratch += [
            pltpu.VMEM((heads, enc, block), jnp.float32),
            pltpu.VMEM((heads, enc, 2 * HEAD), jnp.float32),
        ]
    smem = pl.BlockSpec(memory_space=pltpu.SMEM)
    vmem = pl.BlockSpec(memory_space=pltpu.VMEM)
    return pl.pallas_call(
        functools.partial(attention_kernel, backward, active, width),
        out_shape=shapes,
        in_specs=[smem, smem] + [vmem] * (len(operands) - 2),
        out_specs=[vmem] * len(shapes),
        scratch_shapes=scratch,
        compiler_params=pltpu.CompilerParams(vmem_limit_bytes=VMEM_BYTES),
        cost_estimate=pl.CostEstimate(
            flops=(72 if backward else 32) * rows * enc * feats, bytes_accessed=4 * kv.size,
            transcendentals=rows * enc * heads,
        ),
        name="section_back" if backward else "section_ahead",
    )(*operands)


def totals_kernel(n, part_ref, total_ref, held, send_sem, recv_sem):
    me = lax.axis_index("seq")
    barrier = pltpu.get_barrier_semaphore()

    def greet(k, _):
        pl.semaphore_signal(barrier, inc=1, device_id={"seq": lax.rem(me + k, n)}, device_id_type=MESH)
        return 0

    lax.fori_loop(1, n, greet, 0)
    pl.semaphore_wait(barrier, n - 1)

    def copy(k, slot):
        return pltpu.make_async_remote_copy(
            src_ref=part_ref, dst_ref=held.at[slot], send_sem=send_sem.at[k], recv_sem=recv_sem.at[slot],
            device_id={"seq": lax.rem(me + k, n)}, device_id_type=MESH,
        )

    def send(k, _):
        copy(k, me).start()
        return 0

    lax.fori_loop(1, n, send, 0)

    def take(k, total):
        source = lax.rem(me + k, n)
        copy(k, source).wait_recv()
        return total + held[source]

    total_ref[...] = lax.fori_loop(1, n, take, part_ref[...])

    def finish(k, _):
        copy(k, me).wait_send()
        return 0

    lax.fori_loop(1, n, finish, 0)


def totals(n, part):
    vmem = pl.BlockSpec(memory_space=pltpu.VMEM)
    return pl.pallas_call(
        functools.partial(totals_kernel, n),
        out_shape=jax.ShapeDtypeStruct(part.shape, jnp.float32),
        in_specs=[vmem],
        out_specs=vmem,
        scratch_shapes=[
            pltpu.VMEM((n,) + part.shape, jnp.float32),
            pltpu.SemaphoreType.DMA((n,)),
            pltpu.SemaphoreType.DMA((n,)),
        ],
        compiler_params=pltpu.CompilerParams(collective_id=0, has_side_effects=True),
        name="row_totals",
    )(part)


def exchange_kernel(n, width, ahead, back, *refs):
    refs = list(refs)
    y_ref = refs.pop(0) if ahead else None
    part_ref, cross_ref, x_ref, total_ref = [refs.pop(0) for _ in range(4)] if back else [None] * 4
    x_out, total_out = [refs.pop(0) for _ in range(2)] if ahead else [None] * 2
    g_out = refs.pop(0) if back else None
    if ahead:
        square, held, send_sem, recv_sem, y_send, y_recv = [refs.pop(0) for _ in range(6)]
    if back:
        crosses, grad, cross_send, cross_recv, g_send, g_recv = [refs.pop(0) for _ in range(6)]
    me = lax.axis_index("seq")
    phase = lax.axis_index("phase")
    barrier = pltpu.get_barrier_semaphore()

    def other(k):
        return lax.rem(me + k, n)

    def greet(section, start):
        def signal(k, _):
            pl.semaphore_signal(
                barrier, inc=1, device_id={"phase": section, "seq": other(k)}, device_id_type=MESH
            )
            return 0

        lax.fori_loop(start, n, signal, 0)

    if ahead:
        y_copy = pltpu.make_async_remote_copy(
            src_ref=y_ref, dst_ref=x_out, send_sem=y_send, recv_sem=y_recv,
            device_id={"phase": 1 - phase, "seq": me}, device_id_type=MESH,
        )

        def square_copy(k, slot):
            return pltpu.make_async_remote_copy(
                src_ref=square, dst_ref=held.at[slot], send_sem=send_sem.at[k], recv_sem=recv_sem.at[slot],
                device_id={"phase": 1 - phase, "seq": other(k)}, device_id_type=MESH,
            )

    if back:
        g_copy = pltpu.make_async_remote_copy(
            src_ref=grad, dst_ref=g_out, send_sem=g_send, recv_sem=g_recv,
            device_id={"phase": 1 - phase, "seq": me}, device_id_type=MESH,
        )

        def cross_copy(k, slot):
            return pltpu.make_async_remote_copy(
                src_ref=cross_ref, dst_ref=crosses.at[slot], send_sem=cross_send.at[k],
                recv_sem=cross_recv.at[slot],
                device_id={"phase": phase, "seq": other(k)}, device_id_type=MESH,
            )

    @pl.when(phase == 1)
    def _():
        if back:
            greet(1, 1)
        if ahead:
            greet(0, 0)
        if back:
            pl.semaphore_wait(barrier, n)

            def send(k, _):
                cross_copy(k, me).start()
                return 0

            lax.fori_loop(1, n, send, 0)

            def take(k, total):
                cross_copy(k, other(k)).wait_recv()
                return total + crosses[other(k)]

            cross = lax.fori_loop(1, n, take, cross_ref[...])
            inv = lax.rsqrt(total_ref[...] / width + eps)
            factor = inv * inv * inv * (cross / width)
            grad[...] = (part_ref[...] - x_ref[...].astype(jnp.float32) * factor).astype(jnp.bfloat16)
            g_copy.start()
        if ahead:
            def take_square(k, total):
                square_copy(k, other(k)).wait_recv()
                return total + held[other(k)]

            total_out[...] = lax.fori_loop(0, n, take_square, jnp.zeros(total_out.shape, jnp.float32))
            y_copy.wait_recv()
        if back:
            def finish(k, _):
                cross_copy(k, me).wait_send()
                return 0

            lax.fori_loop(1, n, finish, 0)
            g_copy.wait_send()

    @pl.when(phase == 0)
    def _():
        if back:
            pl.semaphore_signal(barrier, inc=1, device_id={"phase": 1, "seq": me}, device_id_type=MESH)
        if ahead:
            yf = y_ref[...].astype(jnp.float32)
            square[...] = jnp.sum(yf * yf, axis=0, keepdims=True)
            pl.semaphore_wait(barrier, n)

            def send(k, _):
                square_copy(k, me).start()
                return 0

            lax.fori_loop(0, n, send, 0)
            y_copy.start()
        if back:
            g_copy.wait_recv()
        if ahead:
            def finish(k, _):
                square_copy(k, me).wait_send()
                return 0

            lax.fori_loop(0, n, finish, 0)
            y_copy.wait_send()


def exchange(n, width, y=None, back=None):
    vmem = pl.BlockSpec(memory_space=pltpu.VMEM)
    ahead = y is not None
    operands, shapes, scratch = [], [], []
    feats, rows = y.shape if ahead else back[0].shape
    whole = jax.ShapeDtypeStruct((feats, rows), jnp.bfloat16)
    row = jax.ShapeDtypeStruct((1, rows), jnp.float32)
    sems = [pltpu.SemaphoreType.DMA((n,)), pltpu.SemaphoreType.DMA((n,)), pltpu.SemaphoreType.DMA, pltpu.SemaphoreType.DMA]
    if ahead:
        operands.append(y)
        shapes += [whole, row]
        scratch += [pltpu.VMEM((1, rows), jnp.float32), pltpu.VMEM((n, 1, rows), jnp.float32)] + sems
    if back is not None:
        operands += list(back)
        shapes.append(whole)
        scratch += [pltpu.VMEM((n, 1, rows), jnp.float32), pltpu.VMEM((feats, rows), jnp.bfloat16)] + sems
    return pl.pallas_call(
        functools.partial(exchange_kernel, n, width, ahead, back is not None),
        out_shape=shapes,
        in_specs=[vmem] * len(operands),
        out_specs=[vmem] * len(shapes),
        scratch_shapes=scratch,
        compiler_params=pltpu.CompilerParams(
            collective_id=int(ahead) + 2 * int(back is not None), has_side_effects=True
        ),
        name="exchange" + ("_ahead" if ahead else "") + ("_back" if back is not None else ""),
    )(*operands)


def scatter_kernel(kv_ref, out_ref):
    n, _, columns = out_ref.shape
    for j in range(n):
        out_ref[j] = kv_ref[0, 0, :, j * columns:(j + 1) * columns]


def scatter(n, m, enc_kv):
    _, _, rows, columns = enc_kv.shape
    return pl.pallas_call(
        scatter_kernel,
        grid=(1,),
        out_shape=jax.ShapeDtypeStruct((n, rows, columns // n), enc_kv.dtype),
        in_specs=[pl.BlockSpec((1, 1, rows, columns), lambda i: (0, m, 0, 0))],
        out_specs=pl.BlockSpec((n, rows, columns // n), lambda i: (0, 0, 0)),
        compiler_params=pltpu.CompilerParams(vmem_limit_bytes=VMEM_BYTES),
        name="scatter",
    )(enc_kv)


def gather_kernel(*refs):
    *parts, out_ref = refs
    n, _, columns = parts[0].shape
    for m, part in enumerate(parts):
        for j in range(n):
            out_ref[0, m, :, j * columns:(j + 1) * columns] = part[j]


def gather(parts):
    n, rows, columns = parts[0].shape
    tile = 32 if rows % 32 == 0 else rows
    return pl.pallas_call(
        gather_kernel,
        grid=(rows // tile,),
        out_shape=jax.ShapeDtypeStruct((1, len(parts), rows, n * columns), parts[0].dtype),
        in_specs=[pl.BlockSpec((n, tile, columns), lambda i: (0, i, 0))] * len(parts),
        out_specs=pl.BlockSpec((1, len(parts), tile, n * columns), lambda i: (0, 0, i, 0)),
        compiler_params=pltpu.CompilerParams(vmem_limit_bytes=VMEM_BYTES),
        name="gather",
    )(*parts)


def doc_bounds(qseg, kseg):
    block = min(QROWS, qseg.shape[0])
    chunk = min(CHUNK, kseg.shape[0])
    blocks = qseg.reshape(-1, block)
    below = jnp.sum(kseg[None, :] < blocks[:, :1], axis=1)
    upto = jnp.sum(kseg[None, :] <= blocks[:, -1:], axis=1)
    return jnp.stack([below // chunk, (upto + chunk - 1) // chunk], axis=1).reshape(-1).astype(jnp.int32)


def local(n, dec_in, enc_kv, dec_seg, enc_seg, q_gain, o_gain, cotangent):
    phase = lax.axis_index("phase")
    micro, rows, feats = dec_in.shape
    own_enc = enc_kv.shape[2]
    enc = enc_seg.shape[1]
    width = feats * n
    flag = phase.astype(jnp.int32).reshape(1)
    qg = q_gain.reshape(feats, 1)
    og = o_gain.reshape(feats, 1)
    inputs = dec_in.transpose(0, 2, 1)
    wanted = cotangent.transpose(0, 2, 1)
    xf = inputs.astype(jnp.float32)
    first_totals = totals(n, jnp.sum(xf * xf, axis=1))
    scattered = []
    for m in range(micro):
        blocks = scatter(n, m, enc_kv)
        if m > 0:
            blocks, scattered[-1] = lax.optimization_barrier((blocks, scattered[-1]))
        else:
            blocks, first_totals = lax.optimization_barrier((blocks, first_totals))
        scattered.append(lax.all_to_all(blocks, "seq", split_axis=0, concat_axis=0, tiled=True))

    calls, x0s, t0s = [], [], []
    for m in range(micro):
        calls.append(functools.partial(
            attention, width=width, phase=flag, bounds=doc_bounds(dec_seg[m], enc_seg[m]),
            kv=scattered[m].reshape(enc, 2 * feats), kseg=enc_seg[m].reshape(enc, 1),
            qseg=dec_seg[m].reshape(1, rows), qg=qg, og=og,
        ))
        x0s.append(inputs[m])
        t0s.append(first_totals[m].reshape(1, rows))
    outs, grads, gqgs, gogs = [], [], [], []

    def finish(m, y0, first, g0):
        y1, gkv1, gqg1, gog1 = first
        _, gkv0, _, _, gqg0, gog0 = calls[m](True, 0, x=x0s[m], total=t0s[m], g=g0)
        outs.append(jnp.where(phase == 0, y0, y1).T)
        grads.append(jnp.where(phase == 0, gkv0, gkv1).reshape(n, own_enc, 2 * feats))
        gqgs.append(jnp.where(phase == 0, gqg0, gqg1))
        gogs.append(jnp.where(phase == 0, gog0, gog1))

    y0 = calls[0](False, 0, x=x0s[0], total=t0s[0])[0]
    x1, total1 = exchange(n, width, y=y0)
    waiting = None
    for m in range(micro):
        y1, gkv1, part, cross, gqg1, gog1 = calls[m](True, 1, x=x1, total=total1, g=wanted[m])
        if waiting is not None:
            waiting[2], part = lax.optimization_barrier((waiting[2], part))
            finish(m - 1, *waiting)
        waiting = [y0, (y1, gkv1, gqg1, gog1), None]
        if m + 1 < micro:
            x_next, part = lax.optimization_barrier((x0s[m + 1], part))
            y0 = calls[m + 1](False, 0, x=x_next, total=t0s[m + 1])[0]
            x1, total1, waiting[2] = exchange(n, width, y=y0, back=(part, cross, x1, total1))
        else:
            waiting[2] = exchange(n, width, back=(part, cross, x1, total1))[0]
            if grads:
                grads[-1], waiting[2] = lax.optimization_barrier((grads[-1], waiting[2]))
    finish(micro - 1, *waiting)
    returned = []
    for m in range(micro):
        grad = grads[m]
        if returned:
            grad, returned[-1] = lax.optimization_barrier((grad, returned[-1]))
        returned.append(lax.all_to_all(grad, "seq", split_axis=0, concat_axis=0, tiled=True))
    return (
        jnp.stack(outs)[None],
        gather(returned),
        sum(gqgs).reshape(1, feats),
        sum(gogs).reshape(1, feats),
    )


def solution(mesh):
    in_specs = (
        P(None, None, "seq"),
        P("phase", None, "seq", None),
        P(),
        P(),
        P("phase", "seq"),
        P("phase", "seq"),
        P(None, None, "seq"),
    )
    out_specs = (
        P("phase", None, None, "seq"),
        P("phase", None, "seq", None),
        P("phase", "seq"),
        P("phase", "seq"),
    )
    body = functools.partial(local, mesh.shape["seq"])
    return jax.shard_map(body, mesh=mesh, in_specs=in_specs, out_specs=out_specs, check_vma=False)
```

```python
import functools

import jax
import jax.numpy as jnp
from jax import lax
from jax.experimental import pallas as pl
from jax.experimental.pallas import tpu as pltpu
from jax.sharding import PartitionSpec as P

HEAD = 64
QROWS = 256
CHUNK = 256
SCALE = 0.125

eps = 1e-06
neg_big = -1e30
MESH = pl.DeviceIdType.MESH
VMEM_BYTES = 56 * 1024 * 1024


def matmul(a, b):
    return lax.dot_general(a, b, (((1,), (0,)), ((), ())), preferred_element_type=jnp.float32)


def matmul_t(a, b):
    return lax.dot_general(a, b, (((1,), (1,)), ((), ())), preferred_element_type=jnp.float32)


def attention_kernel(backward, width, *refs):
    if backward:
        (bound_ref, kv_ref, kseg_ref, qseg_ref, x_ref, total_ref, qg_ref, og_ref, g_ref,
         y_ref, gkv_ref, part_ref, cross_ref, gqg_ref, gog_ref,
         score_ref, top_ref, kvt_ref, pair_ref, gprob_ref, acc_ref) = refs
    else:
        (bound_ref, kv_ref, kseg_ref, qseg_ref, x_ref, total_ref, qg_ref, og_ref,
         y_ref, score_ref, top_ref, kvt_ref, pair_ref) = refs
    enc = kv_ref.shape[0]
    feats, rows = x_ref.shape
    heads = feats // HEAD
    block = min(QROWS, rows)
    chunk = min(CHUNK, enc)
    every = range(heads)
    lanes = [slice(2 * HEAD * h, 2 * HEAD * (h + 1)) for h in every]
    owns = [slice(HEAD * h, HEAD * (h + 1)) for h in every]

    def place(c):
        return pl.ds(pl.multiple_of(c * chunk, chunk), chunk)

    def work():
        def turn(c, _):
            at = place(c)
            for h in every:
                kvt_ref[h, :, at] = kv_ref[at, lanes[h]].T
                if backward:
                    acc_ref[h, at, :] = jnp.zeros((chunk, 2 * HEAD), jnp.float32)
            return 0

        lax.fori_loop(0, enc // chunk, turn, 0)
        row = jnp.zeros((1, block), jnp.float32)
        tall = jnp.zeros((2 * HEAD, block), jnp.float32)
        blank = jnp.zeros((HEAD, block), jnp.bfloat16)
        for b in range(rows // block):
            cols = slice(b * block, (b + 1) * block)
            low = bound_ref[2 * b]
            high = bound_ref[2 * b + 1]
            inv = lax.rsqrt(total_ref[:, cols] / width + eps)
            qseg = qseg_ref[:, cols]

            def normed_of(h):
                return x_ref[owns[h], cols].astype(jnp.float32) * inv

            for h in every:
                query = (normed_of(h) * qg_ref[owns[h], :]).astype(jnp.bfloat16)
                scaled = (query.astype(jnp.float32) * SCALE).astype(jnp.bfloat16)
                pair_ref[h, :, :block] = jnp.concatenate([scaled, blank], axis=0)
                if backward:
                    grad = (g_ref[owns[h], cols].astype(jnp.float32) * og_ref[owns[h], :]).astype(jnp.bfloat16)
                    pair_ref[h, :, block:] = jnp.concatenate([blank, grad], axis=0)

            def scores(c, carry):
                at = place(c)
                allowed = kseg_ref[at, :] == qseg
                found = []
                for h in every:
                    top, total = carry[h]
                    s = matmul(kv_ref[at, lanes[h]], pair_ref[h, :, :block])
                    s = jnp.where(allowed, s, neg_big)
                    higher = jnp.maximum(top, jnp.max(s, axis=0, keepdims=True))
                    e = jnp.exp(s - higher)
                    score_ref[h, at, :] = e
                    top_ref[h, pl.ds(c, 1), :] = higher
                    found.append((higher, total * jnp.exp(top - higher) + jnp.sum(e, axis=0, keepdims=True)))
                return tuple(found)

            found = lax.fori_loop(low, high, scores, tuple((row + neg_big, row) for h in every))
            tops = [top for top, _ in found]
            shares = [1.0 / total for _, total in found]

            def probs_of(h, c, at):
                return score_ref[h, at, :] * (jnp.exp(top_ref[h, pl.ds(c, 1), :] - tops[h]) * shares[h])

            if not backward:
                def outputs(c, outs):
                    at = place(c)
                    return tuple(
                        outs[h] + matmul(kvt_ref[h, :, at], probs_of(h, c, at).astype(jnp.bfloat16)) for h in every
                    )

                outs = lax.fori_loop(low, high, outputs, tuple(tall for h in every))
                for h in every:
                    xf = x_ref[owns[h], cols].astype(jnp.float32)
                    y_ref[owns[h], cols] = (xf + og_ref[owns[h], :] * outs[h][HEAD:]).astype(jnp.bfloat16)
                continue

            def outputs_and_delta(c, carry):
                at = place(c)
                found = []
                for h in every:
                    out, delta = carry[h]
                    probs = probs_of(h, c, at)
                    score_ref[h, at, :] = probs
                    gprob = matmul(kv_ref[at, lanes[h]], pair_ref[h, :, block:])
                    gprob_ref[h, at, :] = gprob
                    out = out + matmul(kvt_ref[h, :, at], probs.astype(jnp.bfloat16))
                    found.append((out, delta + jnp.sum(probs * gprob, axis=0, keepdims=True)))
                return tuple(found)

            found = lax.fori_loop(low, high, outputs_and_delta, tuple((tall, row) for h in every))
            outs = [out for out, _ in found]
            deltas = [delta for _, delta in found]

            def gradients(c, gqs):
                at = place(c)
                found = []
                for h in every:
                    probs = score_ref[h, at, :]
                    gscore = (probs * (gprob_ref[h, at, :] - deltas[h])).astype(jnp.bfloat16)
                    both = jnp.concatenate([gscore, probs.astype(jnp.bfloat16)], axis=1)
                    acc_ref[h, at, :] += matmul_t(both, pair_ref[h])
                    found.append(gqs[h] + matmul(kvt_ref[h, :, at], gscore))
                return tuple(found)

            gqs = lax.fori_loop(low, high, gradients, tuple(tall for h in every))
            cross = row
            for h in every:
                own = owns[h]
                xf = x_ref[own, cols].astype(jnp.float32)
                gf = g_ref[own, cols].astype(jnp.float32)
                out = outs[h][HEAD:]
                gq = gqs[h][:HEAD] * SCALE
                gn = gq * qg_ref[own, :]
                y_ref[own, cols] = (xf + og_ref[own, :] * out).astype(jnp.bfloat16)
                part_ref[own, cols] = gf + inv * gn
                cross = cross + jnp.sum(gn * xf, axis=0, keepdims=True)
                gqg = jnp.sum(gq * normed_of(h), axis=1, keepdims=True)
                gog = jnp.sum(gf * out, axis=1, keepdims=True)
                gqg_ref[own, :] = gqg if b == 0 else gqg_ref[own, :] + gqg
                gog_ref[own, :] = gog if b == 0 else gog_ref[own, :] + gog
            cross_ref[:, cols] = cross
        if backward:
            def store(c, _):
                at = place(c)
                for h in every:
                    gkv_ref[at, lanes[h]] = acc_ref[h, at, :].astype(jnp.bfloat16)
                return 0

            lax.fori_loop(0, enc // chunk, store, 0)

    work()


def attention(backward, width, bounds, kv, kseg, qseg, x, total, qg, og, g=None):
    enc = kv.shape[0]
    feats, rows = x.shape
    block = min(QROWS, rows)
    shapes = [jax.ShapeDtypeStruct((feats, rows), jnp.bfloat16)]
    heads = feats // HEAD
    scratch = [
        pltpu.VMEM((heads, enc, block), jnp.float32),
        pltpu.VMEM((heads, max(8, enc // min(CHUNK, enc)), block), jnp.float32),
        pltpu.VMEM((heads, 2 * HEAD, enc), jnp.bfloat16),
        pltpu.VMEM((heads, 2 * HEAD, 2 * block if backward else block), jnp.bfloat16),
    ]
    operands = [bounds, kv, kseg, qseg, x, total, qg, og]
    if backward:
        operands.append(g)
        shapes += [
            jax.ShapeDtypeStruct(kv.shape, jnp.bfloat16),
            jax.ShapeDtypeStruct((feats, rows), jnp.float32),
            jax.ShapeDtypeStruct((1, rows), jnp.float32),
            jax.ShapeDtypeStruct((feats, 1), jnp.float32),
            jax.ShapeDtypeStruct((feats, 1), jnp.float32),
        ]
        scratch += [
            pltpu.VMEM((heads, enc, block), jnp.float32),
            pltpu.VMEM((heads, enc, 2 * HEAD), jnp.float32),
        ]
    smem = pl.BlockSpec(memory_space=pltpu.SMEM)
    vmem = pl.BlockSpec(memory_space=pltpu.VMEM)
    return pl.pallas_call(
        functools.partial(attention_kernel, backward, width),
        out_shape=shapes,
        in_specs=[smem] + [vmem] * (len(operands) - 1),
        out_specs=[vmem] * len(shapes),
        scratch_shapes=scratch,
        compiler_params=pltpu.CompilerParams(vmem_limit_bytes=VMEM_BYTES),
        cost_estimate=pl.CostEstimate(
            flops=(72 if backward else 32) * rows * enc * feats, bytes_accessed=4 * kv.size,
            transcendentals=rows * enc * heads,
        ),
        name="section_back" if backward else "section_ahead",
    )(*operands)


def totals_kernel(n, part_ref, total_ref, held, send_sem, recv_sem):
    me = lax.axis_index("seq")
    barrier = pltpu.get_barrier_semaphore()

    def greet(k, _):
        pl.semaphore_signal(barrier, inc=1, device_id={"seq": lax.rem(me + k, n)}, device_id_type=MESH)
        return 0

    lax.fori_loop(1, n, greet, 0)
    pl.semaphore_wait(barrier, n - 1)

    def copy(k, slot):
        return pltpu.make_async_remote_copy(
            src_ref=part_ref, dst_ref=held.at[slot], send_sem=send_sem.at[k], recv_sem=recv_sem.at[slot],
            device_id={"seq": lax.rem(me + k, n)}, device_id_type=MESH,
        )

    def send(k, _):
        copy(k, me).start()
        return 0

    lax.fori_loop(1, n, send, 0)

    def take(k, total):
        source = lax.rem(me + k, n)
        copy(k, source).wait_recv()
        return total + held[source]

    total_ref[...] = lax.fori_loop(1, n, take, part_ref[...])

    def finish(k, _):
        copy(k, me).wait_send()
        return 0

    lax.fori_loop(1, n, finish, 0)


def totals(n, part):
    vmem = pl.BlockSpec(memory_space=pltpu.VMEM)
    return pl.pallas_call(
        functools.partial(totals_kernel, n),
        out_shape=jax.ShapeDtypeStruct(part.shape, jnp.float32),
        in_specs=[vmem],
        out_specs=vmem,
        scratch_shapes=[
            pltpu.VMEM((n,) + part.shape, jnp.float32),
            pltpu.SemaphoreType.DMA((n,)),
            pltpu.SemaphoreType.DMA((n,)),
        ],
        compiler_params=pltpu.CompilerParams(collective_id=0, has_side_effects=True),
        name="row_totals",
    )(part)


def exchange_kernel(n, width, ahead, back, *refs):
    refs = list(refs)
    y_ref = refs.pop(0) if ahead else None
    part_ref, cross_ref, x_ref, total_ref = [refs.pop(0) for _ in range(4)] if back else [None] * 4
    x_out, total_out = [refs.pop(0) for _ in range(2)] if ahead else [None] * 2
    g_out = refs.pop(0) if back else None
    if ahead:
        square, held, send_sem, recv_sem, y_send, y_recv = [refs.pop(0) for _ in range(6)]
    if back:
        crosses, grad, cross_send, cross_recv, g_send, g_recv = [refs.pop(0) for _ in range(6)]
    me = lax.axis_index("seq")
    phase = lax.axis_index("phase")
    barrier = pltpu.get_barrier_semaphore()

    def other(k):
        return lax.rem(me + k, n)

    def greet(section, start):
        def signal(k, _):
            pl.semaphore_signal(
                barrier, inc=1, device_id={"phase": section, "seq": other(k)}, device_id_type=MESH
            )
            return 0

        lax.fori_loop(start, n, signal, 0)

    if ahead:
        y_copy = pltpu.make_async_remote_copy(
            src_ref=y_ref, dst_ref=x_out, send_sem=y_send, recv_sem=y_recv,
            device_id={"phase": 1 - phase, "seq": me}, device_id_type=MESH,
        )

        def square_copy(k, slot):
            return pltpu.make_async_remote_copy(
                src_ref=square, dst_ref=held.at[slot], send_sem=send_sem.at[k], recv_sem=recv_sem.at[slot],
                device_id={"phase": 1 - phase, "seq": other(k)}, device_id_type=MESH,
            )

    if back:
        g_copy = pltpu.make_async_remote_copy(
            src_ref=grad, dst_ref=g_out, send_sem=g_send, recv_sem=g_recv,
            device_id={"phase": 1 - phase, "seq": me}, device_id_type=MESH,
        )

        def cross_copy(k, slot):
            return pltpu.make_async_remote_copy(
                src_ref=cross_ref, dst_ref=crosses.at[slot], send_sem=cross_send.at[k],
                recv_sem=cross_recv.at[slot],
                device_id={"phase": phase, "seq": other(k)}, device_id_type=MESH,
            )

    @pl.when(phase == 1)
    def _():
        if back:
            greet(1, 1)
        if ahead:
            greet(0, 0)
        if back:
            pl.semaphore_wait(barrier, n)

            def send(k, _):
                cross_copy(k, me).start()
                return 0

            lax.fori_loop(1, n, send, 0)

            def take(k, total):
                cross_copy(k, other(k)).wait_recv()
                return total + crosses[other(k)]

            cross = lax.fori_loop(1, n, take, cross_ref[...])
            inv = lax.rsqrt(total_ref[...] / width + eps)
            factor = inv * inv * inv * (cross / width)
            grad[...] = (part_ref[...] - x_ref[...].astype(jnp.float32) * factor).astype(jnp.bfloat16)
            g_copy.start()
        if ahead:
            def take_square(k, total):
                square_copy(k, other(k)).wait_recv()
                return total + held[other(k)]

            total_out[...] = lax.fori_loop(0, n, take_square, jnp.zeros(total_out.shape, jnp.float32))
            y_copy.wait_recv()
        if back:
            def finish(k, _):
                cross_copy(k, me).wait_send()
                return 0

            lax.fori_loop(1, n, finish, 0)
            g_copy.wait_send()

    @pl.when(phase == 0)
    def _():
        if back:
            pl.semaphore_signal(barrier, inc=1, device_id={"phase": 1, "seq": me}, device_id_type=MESH)
        if ahead:
            yf = y_ref[...].astype(jnp.float32)
            square[...] = jnp.sum(yf * yf, axis=0, keepdims=True)
            pl.semaphore_wait(barrier, n)

            def send(k, _):
                square_copy(k, me).start()
                return 0

            lax.fori_loop(0, n, send, 0)
            y_copy.start()
        if back:
            g_copy.wait_recv()
        if ahead:
            def finish(k, _):
                square_copy(k, me).wait_send()
                return 0

            lax.fori_loop(0, n, finish, 0)
            y_copy.wait_send()


def exchange(n, width, y=None, back=None):
    vmem = pl.BlockSpec(memory_space=pltpu.VMEM)
    ahead = y is not None
    operands, shapes, scratch = [], [], []
    feats, rows = y.shape if ahead else back[0].shape
    whole = jax.ShapeDtypeStruct((feats, rows), jnp.bfloat16)
    row = jax.ShapeDtypeStruct((1, rows), jnp.float32)
    sems = [pltpu.SemaphoreType.DMA((n,)), pltpu.SemaphoreType.DMA((n,)), pltpu.SemaphoreType.DMA, pltpu.SemaphoreType.DMA]
    if ahead:
        operands.append(y)
        shapes += [whole, row]
        scratch += [pltpu.VMEM((1, rows), jnp.float32), pltpu.VMEM((n, 1, rows), jnp.float32)] + sems
    if back is not None:
        operands += list(back)
        shapes.append(whole)
        scratch += [pltpu.VMEM((n, 1, rows), jnp.float32), pltpu.VMEM((feats, rows), jnp.bfloat16)] + sems
    return pl.pallas_call(
        functools.partial(exchange_kernel, n, width, ahead, back is not None),
        out_shape=shapes,
        in_specs=[vmem] * len(operands),
        out_specs=[vmem] * len(shapes),
        scratch_shapes=scratch,
        compiler_params=pltpu.CompilerParams(
            collective_id=int(ahead) + 2 * int(back is not None), has_side_effects=True
        ),
        name="exchange" + ("_ahead" if ahead else "") + ("_back" if back is not None else ""),
    )(*operands)


def scatter_kernel(kv_ref, out_ref):
    n, _, columns = out_ref.shape
    for j in range(n):
        out_ref[j] = kv_ref[0, 0, :, j * columns:(j + 1) * columns]


def scatter(n, m, enc_kv):
    _, _, rows, columns = enc_kv.shape
    return pl.pallas_call(
        scatter_kernel,
        grid=(1,),
        out_shape=jax.ShapeDtypeStruct((n, rows, columns // n), enc_kv.dtype),
        in_specs=[pl.BlockSpec((1, 1, rows, columns), lambda i: (0, m, 0, 0))],
        out_specs=pl.BlockSpec((n, rows, columns // n), lambda i: (0, 0, 0)),
        compiler_params=pltpu.CompilerParams(vmem_limit_bytes=VMEM_BYTES),
        name="scatter",
    )(enc_kv)


def gather_kernel(*refs):
    *parts, out_ref = refs
    n, _, columns = parts[0].shape
    for m, part in enumerate(parts):
        for j in range(n):
            out_ref[0, m, :, j * columns:(j + 1) * columns] = part[j]


def gather(parts):
    n, rows, columns = parts[0].shape
    tile = 32 if rows % 32 == 0 else rows
    return pl.pallas_call(
        gather_kernel,
        grid=(rows // tile,),
        out_shape=jax.ShapeDtypeStruct((1, len(parts), rows, n * columns), parts[0].dtype),
        in_specs=[pl.BlockSpec((n, tile, columns), lambda i: (0, i, 0))] * len(parts),
        out_specs=pl.BlockSpec((1, len(parts), tile, n * columns), lambda i: (0, 0, i, 0)),
        compiler_params=pltpu.CompilerParams(vmem_limit_bytes=VMEM_BYTES),
        name="gather",
    )(*parts)


def doc_bounds(qseg, kseg):
    block = min(QROWS, qseg.shape[0])
    chunk = min(CHUNK, kseg.shape[0])
    blocks = qseg.reshape(-1, block)
    below = jnp.sum(kseg[None, :] < blocks[:, :1], axis=1)
    upto = jnp.sum(kseg[None, :] <= blocks[:, -1:], axis=1)
    return jnp.stack([below // chunk, (upto + chunk - 1) // chunk], axis=1).reshape(-1).astype(jnp.int32)


def local(n, dec_in, enc_kv, dec_seg, enc_seg, q_gain, o_gain, cotangent):
    phase = lax.axis_index("phase")
    micro, rows, feats = dec_in.shape
    own_enc = enc_kv.shape[2]
    enc = enc_seg.shape[1]
    width = feats * n
    qg = q_gain.reshape(feats, 1)
    og = o_gain.reshape(feats, 1)
    inputs = dec_in.transpose(0, 2, 1)
    wanted = cotangent.transpose(0, 2, 1)
    xf = inputs.astype(jnp.float32)
    first_totals = totals(n, jnp.sum(xf * xf, axis=1))
    scattered = []
    for m in range(micro):
        blocks = scatter(n, m, enc_kv)
        if m > 0:
            blocks, scattered[-1] = lax.optimization_barrier((blocks, scattered[-1]))
        else:
            blocks, first_totals = lax.optimization_barrier((blocks, first_totals))
        scattered.append(lax.all_to_all(blocks, "seq", split_axis=0, concat_axis=0, tiled=True))

    calls, x0s, t0s = [], [], []
    for m in range(micro):
        calls.append(functools.partial(
            attention, width=width, bounds=doc_bounds(dec_seg[m], enc_seg[m]),
            kv=scattered[m].reshape(enc, 2 * feats), kseg=enc_seg[m].reshape(enc, 1),
            qseg=dec_seg[m].reshape(1, rows), qg=qg, og=og,
        ))
        x0s.append(inputs[m])
        t0s.append(first_totals[m].reshape(1, rows))
    outs, grads, gqgs, gogs = [], [], [], []

    def section_ahead(m, x0):
        def run():
            return calls[m](False, x=x0, total=t0s[m])[0]

        return lax.cond(phase == 0, run, lambda: x0)

    def section_back(m, x1, total1):
        def run():
            return tuple(calls[m](True, x=x1, total=total1, g=wanted[m]))

        def rest():
            column = jnp.zeros((feats, 1), jnp.float32)
            return (x1, calls[m].keywords["kv"], jnp.zeros((feats, rows), jnp.float32), total1, column, column)

        return lax.cond(phase == 1, run, rest)

    def finish(m, y0, first, g0):
        def run():
            _, gkv0, _, _, gqg0, gog0 = calls[m](True, x=x0s[m], total=t0s[m], g=g0)
            return (gkv0, gqg0, gog0)

        y1, gkv1, gqg1, gog1 = first
        outs.append(jnp.where(phase == 0, y0, y1).T)
        gkv, gqg, gog = lax.cond(phase == 0, run, lambda: (gkv1, gqg1, gog1))
        grads.append(gkv.reshape(n, own_enc, 2 * feats))
        gqgs.append(gqg)
        gogs.append(gog)

    y0 = section_ahead(0, x0s[0])
    x1, total1 = exchange(n, width, y=y0)
    waiting = None
    for m in range(micro):
        y1, gkv1, part, cross, gqg1, gog1 = section_back(m, x1, total1)
        if waiting is not None:
            waiting[2], part = lax.optimization_barrier((waiting[2], part))
            finish(m - 1, *waiting)
        waiting = [y0, (y1, gkv1, gqg1, gog1), None]
        if m + 1 < micro:
            x_next, part = lax.optimization_barrier((x0s[m + 1], part))
            y0 = section_ahead(m + 1, x_next)
            x1, total1, waiting[2] = exchange(n, width, y=y0, back=(part, cross, x1, total1))
        else:
            if grads:
                cross, grads[-1] = lax.optimization_barrier((cross, grads[-1]))
            waiting[2] = exchange(n, width, back=(part, cross, x1, total1))[0]
            if grads:
                grads[-1], waiting[2] = lax.optimization_barrier((grads[-1], waiting[2]))
    finish(micro - 1, *waiting)
    returned = []
    for m in range(micro):
        grad = grads[m]
        if returned:
            grad, returned[-1] = lax.optimization_barrier((grad, returned[-1]))
        returned.append(lax.all_to_all(grad, "seq", split_axis=0, concat_axis=0, tiled=True))
    return (
        jnp.stack(outs)[None],
        gather(returned),
        sum(gqgs).reshape(1, feats),
        sum(gogs).reshape(1, feats),
    )


def solution(mesh):
    in_specs = (
        P(None, None, "seq"),
        P("phase", None, "seq", None),
        P(),
        P(),
        P("phase", "seq"),
        P("phase", "seq"),
        P(None, None, "seq"),
    )
    out_specs = (
        P("phase", None, None, "seq"),
        P("phase", None, "seq", None),
        P("phase", "seq"),
        P("phase", "seq"),
    )
    body = functools.partial(local, mesh.shape["seq"])
    return jax.shard_map(body, mesh=mesh, in_specs=in_specs, out_specs=out_specs, check_vma=False)
```
